128 devices in a mesh: row: 16 (over z, y), col: 8 (over x, core).
Axes of the slice: x: 4, y: 4, z: 4, core: 2. Of those that a mesh axis runs over, the one named last changes fastest.
Arguments:
- rhs_leaf: bfloat16 [128, 2048, 128], P(('row', 'col')), may hold values from -6 to 6
- rhs_sep: bfloat16 [2048, 128], P('col'), may hold values from -6 to 6
- leaf_sizes: int32 [128], P(('row', 'col')), may hold values from 512 to 2048, as said below
- off_blocks: int32 [128, 4], P(('row', 'col')), may hold values from 0 to 15, as said below
- linv_leaf: bfloat16 [128, 2048, 2048], P(('row', 'col')), as said below
- uinv_leaf: bfloat16 [128, 2048, 2048], P(('row', 'col')), as said below
- l_off: bfloat16 [128, 512, 2048], P(('row', 'col')), may hold values from -0.0234375 to 0.0234375
- u_off: bfloat16 [128, 2048, 512], P(('row', 'col')), may hold values from -0.25 to 0.25
- linv_sep: bfloat16 [2048, 2048], P('row', 'col'), as said below
- uinv_sep: bfloat16 [2048, 2048], P('row', 'col'), as said below
Outputs:
- solved_leaf: bfloat16 [128, 2048, 128], P(('row', 'col'))
- solved_sep: bfloat16 [2048, 128], P('row')
The draws below stay inside these ranges and needn't reach their ends.
Inputs may be any that keep to these rules, and one draw needn't show every extreme that they name: `leaf_sizes`: between 512 and 2048; the first leaf has exactly 2048. `off_blocks`: the 4 blocks of each leaf are different. `linv_leaf`: lower triangular, diagonal between 0.5 and 1.5. `uinv_leaf`: upper triangular, diagonal between 0.5 and 1.5. `linv_sep`: lower triangular, diagonal between 0.5 and 1.5. `uinv_sep`: upper triangular, diagonal between 0.5 and 1.5.
All inputs are finite; a program needn't handle non-finite values.
Results may differ from the reference program's by a relative error of at most 0.013.
Values may be sent and summed in bfloat16 or wider, within the bound.
A program may use at most 64 MiB of HBM per device.

```python
import jax
import jax.numpy as jnp
from jax import lax

W = 2048
S = 2048
NRHS = 128
BLK = 128
KB = 4
NLEAF = 128
SB = 16


def shape_triangle(noise, diagonal_values, lower_side):
    order = noise.shape[-1]
    row_ids = jnp.arange(order)[:, None]
    col_ids = jnp.arange(order)[None, :]
    if lower_side:
        strict = col_ids < row_ids
    else:
        strict = col_ids > row_ids
    spread = order ** (-0.5)
    values = jnp.where(strict, noise * spread, 0.0)
    values = jnp.where(row_ids == col_ids, diagonal_values, values)
    return values.astype(jnp.float32)


def triangle_draw(key, dims_shape, lower_side):
    first_key, second_key = jax.random.split(key)
    noise = jax.random.normal(first_key, dims_shape, jnp.float32)
    diagonal_values = jax.random.uniform(second_key, dims_shape[:-1] + (1,), jnp.float32, 0.5, 1.5)
    return shape_triangle(noise, diagonal_values, lower_side)


def draw_leaf_sizes(key, part):
    key = jax.random.fold_in(key, 1)
    values = jax.random.randint(key, (NLEAF,), W // 4, W + 1, jnp.int32)
    return values.at[0].set(W)


def draw_off_blocks(key, part):
    key = jax.random.fold_in(key, 2)
    leaf_keys = jax.random.split(key, NLEAF)
    orders = jax.vmap(lambda one_key: jax.random.permutation(one_key, SB))(leaf_keys)
    return orders[:, :KB].astype(jnp.int32)


def draw_linv_leaf(key, part):
    key = jax.random.fold_in(key, 3)
    return triangle_draw(key, (NLEAF, W, W), True).astype(jnp.bfloat16)


def draw_uinv_leaf(key, part):
    key = jax.random.fold_in(key, 4)
    return triangle_draw(key, (NLEAF, W, W), False).astype(jnp.bfloat16)


def draw_linv_sep(key, part):
    key = jax.random.fold_in(key, 5)
    return triangle_draw(key, (S, S), True).astype(jnp.bfloat16)


def draw_uinv_sep(key, part):
    key = jax.random.fold_in(key, 6)
    return triangle_draw(key, (S, S), False).astype(jnp.bfloat16)


def block_scale(rng, shape, cuts, least, high):
    gain, own = 1.0, jax.random.fold_in(rng, 6)
    for axis_at, blocks in cuts:
        steps = jnp.exp(jax.random.uniform(jax.random.fold_in(own, axis_at), (blocks,), jnp.float32, least / len(cuts), high / len(cuts)))
        gain = gain * jnp.repeat(steps, shape[axis_at] // blocks).reshape([-1 if axis == axis_at else 1 for axis in range(len(shape))])
    return gain


def bell_draw(own_key, shape, scale, limit, shards=(), kind=jnp.bfloat16):
    factor_of = block_scale(own_key, shape, shards, -0.22, 0.18) if shards else 1.0
    values = jax.random.normal(own_key, shape, jnp.float32) * scale * factor_of
    return jnp.minimum(jnp.maximum(values, -limit), limit).astype(kind)


def setup_inputs(seed: int = 0) -> dict:
    arg_keys = jax.random.split(jax.random.key(seed), 11)
    rhs_leaf = bell_draw(arg_keys[0], (NLEAF, W, NRHS), 1.0, 6.0, ((0, 128),))
    rhs_sep = bell_draw(arg_keys[1], (S, NRHS), 1.0, 6.0, ((0, 8),))
    leaf_sizes = draw_leaf_sizes(jax.random.fold_in(arg_keys[10], 71), 0)
    off_blocks = draw_off_blocks(jax.random.fold_in(arg_keys[10], 71), 0)
    linv_leaf = draw_linv_leaf(jax.random.fold_in(arg_keys[10], 71), 0)
    uinv_leaf = draw_uinv_leaf(jax.random.fold_in(arg_keys[10], 71), 0)
    l_off = bell_draw(arg_keys[6], (NLEAF, KB * BLK, W), (W * NLEAF * KB // SB) ** -0.5, 0.0234375, ((0, 128),))
    u_off = bell_draw(arg_keys[7], (NLEAF, W, KB * BLK), (KB * BLK) ** -0.5, 0.25, ((0, 128),))
    linv_sep = draw_linv_sep(jax.random.fold_in(arg_keys[10], 71), 0)
    uinv_sep = draw_uinv_sep(jax.random.fold_in(arg_keys[10], 71), 0)
    return dict(rhs_leaf=rhs_leaf, rhs_sep=rhs_sep, leaf_sizes=leaf_sizes, off_blocks=off_blocks, linv_leaf=linv_leaf, uinv_leaf=uinv_leaf, l_off=l_off, u_off=u_off, linv_sep=linv_sep, uinv_sep=uinv_sep)


def reference(rhs_leaf, rhs_sep, leaf_sizes, off_blocks, linv_leaf, uinv_leaf, l_off, u_off, linv_sep, uinv_sep):
    positions = jnp.arange(W, dtype=jnp.int32)

    def forward_leaf(carry, items):
        rhs_one, size_one, blocks_one, linv_one, loff_one = items
        keep_rows = (positions < size_one)[:, None]
        masked = jnp.where(keep_rows, rhs_one, jnp.zeros_like(rhs_one))
        forward = jnp.dot(linv_one, masked, preferred_element_type=jnp.float32)
        forward = jnp.where(keep_rows, forward, 0.0).astype(jnp.bfloat16)
        updates = jnp.dot(loff_one, forward, preferred_element_type=jnp.float32)
        carry = carry.at[blocks_one].add(updates.reshape(KB, BLK, NRHS))
        return carry, forward

    start_sum = jnp.zeros((SB, BLK, NRHS), jnp.float32)
    coupled_sum, forward_all = lax.scan(forward_leaf, start_sum, (rhs_leaf, leaf_sizes, off_blocks, linv_leaf, l_off))
    sep_rhs = (rhs_sep.astype(jnp.float32) - coupled_sum.reshape(S, NRHS)).astype(jnp.bfloat16)
    sep_forward = jnp.dot(linv_sep, sep_rhs, preferred_element_type=jnp.float32).astype(jnp.bfloat16)
    solved_sep = jnp.dot(uinv_sep, sep_forward, preferred_element_type=jnp.float32).astype(jnp.bfloat16)
    sep_blocks = solved_sep.reshape(SB, BLK, NRHS)

    def backward_leaf(items):
        forward, size_one, blocks_one, uinv_one, uoff_one = items
        keep_rows = (positions < size_one)[:, None]
        coupled = sep_blocks[blocks_one].reshape(KB * BLK, NRHS)
        residue = forward.astype(jnp.float32) - jnp.dot(uoff_one, coupled, preferred_element_type=jnp.float32)
        residue = jnp.where(keep_rows, residue, 0.0).astype(jnp.bfloat16)
        solved = jnp.dot(uinv_one, residue, preferred_element_type=jnp.float32)
        return jnp.where(keep_rows, solved, 0.0).astype(jnp.bfloat16)

    solved_leaf = lax.map(backward_leaf, (forward_all, leaf_sizes, off_blocks, uinv_leaf, u_off))
    return solved_leaf, solved_sep
```

```python
import jax
import jax.numpy as jnp
from jax import lax
from jax.experimental import pallas as pl
from jax.experimental.pallas import tpu as pltpu
from jax.sharding import PartitionSpec as P

MESH = pl.DeviceIdType.MESH
W = 2048
NR = 128
BLK = 128
KB = 4
TB = 256
NT = W // TB
BF = jnp.bfloat16
F32 = jnp.float32
CLASSES = ((96, 64, "xyz"), (0, 48, "yzx"), (48, 48, "zxy"))
SLOT = 160


def dot(a, b):
    return jnp.dot(a, b, preferred_element_type=F32)


def kernel(
    sizes, offs, rhs_h, rsep_h, linv_h, uinv_h, loff_h, uoff_h, lsep_h, usep_h,
    out_h, osep_h,
    linv, uinv, loff, rhs, mix, gmat, fsol, upd, slots, rsep,
    half, recv_half, pieces, rs_in, xs, pf_send, pf_recv, fwd_sep, ps, pr, coupled, obuf, osep,
    s_rhs, s_linv, s_loff, s_uinv, s_uoff, s_own, s_diag, s_rsep, s_out, s_osep,
    ph_send, ph_recv, dg_send, dg_recv, core_send, core_recv, rs_send, rs_recv, ag_send, ag_recv,
    sem_a, sem_b,
):
    row, col = lax.axis_index("row"), lax.axis_index("col")
    z, y = row // 4, row % 4
    x, k = col // 2, col % 2
    other = 1 - k
    chip = z * 16 + y * 4 + x
    size = sizes[0]
    partner = (row, x * 2 + other)

    def line(dim, step):
        if dim == "z":
            return (((z + step) % 4) * 4 + y, col)
        if dim == "y":
            return (z * 4 + (y + step) % 4, col)
        return (row, ((x + step) % 4) * 2 + k)

    def wait_bytes(ref, sem):
        pltpu.make_async_copy(ref, ref, sem).wait()

    def keep(start, rows, cols):
        return lax.broadcasted_iota(jnp.int32, (rows, cols), 0) + start < size

    barrier = pltpu.get_barrier_semaphore()
    pl.semaphore_signal(barrier, inc=1, device_id=partner, device_id_type=MESH)
    for dim in "xyz":
        for step in (1, 2, 3):
            pl.semaphore_signal(barrier, inc=1, device_id=line(dim, step), device_id_type=MESH)

    def rows_of(i):
        return pl.ds(TB * i, TB)

    pltpu.make_async_copy(rhs_h.at[0], rhs, s_rhs).start()
    own = slots.at[z, y, x, pl.ds(0, BLK)]

    def load_front(i):
        pltpu.make_async_copy(
            linv_h.at[0, rows_of(i), pl.ds(0, TB * (i + 1))],
            linv.at[rows_of(i), pl.ds(0, TB * (i + 1))], s_linv.at[i]).start()
        pltpu.make_async_copy(
            loff_h.at[0, :, rows_of(i)], loff.at[:, rows_of(i)], s_loff.at[i]).start()

    load_front(7)

    @pl.when(x <= z)
    def _():
        pltpu.make_async_copy(lsep_h, own, s_own).start()

    @pl.when(x > z)
    def _():
        pltpu.make_async_copy(usep_h, own, s_own).start()

    @pl.when(x == z)
    def _():
        for j in range(4):
            pltpu.make_async_copy(
                usep_h.at[pl.ds(32 * j, 32)], slots.at[z, y, j, pl.ds(BLK, 32)], s_diag).start()

    for i in range(6, -1, -1):
        load_front(i)
    pltpu.make_async_copy(rsep_h, rsep, s_rsep).start()

    wait_bytes(rhs, s_rhs)
    for i in range(NT):
        part = rhs[rows_of(i), :].astype(F32)
        rhs[rows_of(i), :] = jnp.where(keep(TB * i, TB, NR), part, 0.0).astype(BF)

    total = [None]

    def front(i):
        span = pl.ds(0, TB * (i + 1))
        wait_bytes(linv.at[rows_of(i), span], s_linv.at[i])
        part = dot(linv[rows_of(i), span], rhs[span, :])
        part = jnp.where(keep(TB * i, TB, NR), part, 0.0).astype(BF)
        mix[rows_of(i), pl.ds(KB * BLK, NR)] = part
        wait_bytes(loff.at[:, rows_of(i)], s_loff.at[i])
        term = dot(loff[:, rows_of(i)], part)
        total[0] = term if total[0] is None else total[0] + term

    def region(ph, order, first, rows):
        have = order[:ph]
        return slots.at[
            slice(None) if "z" in have else z,
            slice(None) if "y" in have else y,
            slice(None) if "x" in have else x,
            pl.ds(first, rows)]

    def three(ph, first, rows):
        if ph == 0:
            return slots.at[0, 0, pl.ds(0, 3), pl.ds(first, rows)]
        if ph == 1:
            return slots.at[0, pl.ds(0, 3), :, pl.ds(first, rows)]
        return slots.at[pl.ds(0, 3), :, :, pl.ds(first, rows)]

    def span_of(ph, cl):
        first, rows, order = CLASSES[cl]
        if ph == 0 and cl == 0:
            rows = BLK - first
        return first, rows, order

    def phase_start(ph):
        for cl in range(3):
            first, rows, order = span_of(ph, cl)
            ref = region(ph, order, first, rows)
            for step in (2, 1, 3):
                pltpu.make_async_remote_copy(
                    src_ref=ref, dst_ref=ref, send_sem=ph_send.at[ph, cl], recv_sem=ph_recv.at[ph, cl],
                    device_id=line(order[ph], step), device_id_type=MESH).start()
        if ph == 0:
            @pl.when(x == z)
            def _():
                ref = slots.at[z, y, :, pl.ds(BLK, 32)]
                for step in (2, 1, 3):
                    pltpu.make_async_remote_copy(
                        src_ref=ref, dst_ref=ref, send_sem=dg_send, recv_sem=dg_recv,
                        device_id=line("x", step), device_id_type=MESH).start()

    def phase_wait(ph):
        for cl in range(3):
            first, rows, _ = span_of(ph, cl)
            wait_bytes(three(ph, first, rows), ph_recv.at[ph, cl])
        if ph == 0:
            @pl.when(x != z)
            def _():
                wait_bytes(slots.at[0, 0, :, pl.ds(BLK, 32)], dg_recv)

    def phase_drain(ph):
        for cl in range(3):
            first, rows, _ = span_of(ph, cl)
            wait_bytes(three(ph, first, rows), ph_send.at[ph, cl])
        if ph == 0:
            @pl.when(x == z)
            def _():
                wait_bytes(slots.at[0, pl.ds(0, 3), :, pl.ds(BLK, 32)], dg_send)

    front(7)
    wait_bytes(own, s_own)

    @pl.when(x == z)
    def _():
        wait_bytes(slots.at[0, 0, :, pl.ds(BLK, 32)], s_diag)

    pl.semaphore_wait(barrier, 10)
    for step in (1, 2, 3):
        pl.semaphore_signal(sem_a, inc=1, device_id=line("x", step), device_id_type=MESH)
    phase_start(0)
    for i in (6, 5, 4):
        front(i)
    pltpu.make_async_copy(
        uoff_h.at[0], mix.at[:, pl.ds(0, KB * BLK)], s_uoff).start()
    for i in range(NT):
        span = pl.ds(TB * i, W - TB * i)
        pltpu.make_async_copy(
            uinv_h.at[0, rows_of(i), span], uinv.at[rows_of(i), span], s_uinv.at[i]).start()
    pl.semaphore_wait(sem_a, 3)
    for step in (1, 2, 3):
        pl.semaphore_signal(sem_b, inc=1, device_id=line("y", step), device_id_type=MESH)
    for i in (3, 2, 1, 0):
        front(i)

    for j in range(KB):
        upd[j] = total[0][BLK * j:BLK * (j + 1), :].reshape(8, 16, NR).astype(BF)
    upd[KB] = jnp.zeros((8, 16, NR), BF)
    named = [offs[0, j] for j in range(KB)]

    def block(s):
        at = jnp.int32(KB)
        for j in range(KB):
            at = jnp.where(named[j] == s, j, at)
        return upd[at]

    for c4 in range(4):
        for b in range(2):
            half[c4, pl.ds(8 * b, 8)] = block(4 * c4 + 2 * other + b)
    swap = pltpu.make_async_remote_copy(
        src_ref=half, dst_ref=recv_half, send_sem=core_send.at[0], recv_sem=core_recv.at[0],
        device_id=partner, device_id_type=MESH)
    swap.start()
    phase_wait(0)
    phase_start(1)
    pl.semaphore_wait(sem_b, 3)
    swap.wait_recv()
    for c4 in range(4):
        for b in range(2):
            mine = block(4 * c4 + 2 * k + b).astype(F32)
            got = recv_half[c4, pl.ds(8 * b, 8)].astype(F32)
            pieces[pl.ds(16 * c4 + 8 * b, 8)] = (mine + got).astype(BF)

    def peer(i):
        dz, dy, dx = (i // 16 + 2) % 4, (i // 4 + 2) % 4, (i + 2) % 4
        pz, py, px = (z + dz) % 4, (y + dy) % 4, (x + dx) % 4
        return pz * 4 + py, px

    def rs_body(i, carry):
        @pl.when(i != 42)
        def _():
            prow, px = peer(i)
            pltpu.make_async_remote_copy(
                src_ref=pieces.at[px * 16 + prow], dst_ref=rs_in.at[chip], send_sem=rs_send, recv_sem=rs_recv,
                device_id=(prow, px * 2 + k), device_id_type=MESH).start()
        return carry

    lax.fori_loop(0, 64, rs_body, 0)
    rs_in[chip] = pieces[x * 16 + row]

    wait_bytes(mix.at[:, pl.ds(0, KB * BLK)], s_uoff)
    for i in range(NT):
        part = mix[rows_of(i), pl.ds(0, KB * BLK)].astype(F32)
        mix[rows_of(i), pl.ds(0, KB * BLK)] = jnp.where(keep(TB * i, TB, KB * BLK), part, 0.0).astype(BF)

    def back(i):
        span = pl.ds(TB * i, W - TB * i)
        wait_bytes(uinv.at[rows_of(i), span], s_uinv.at[i])
        gmat[rows_of(i), :] = dot(uinv[rows_of(i), span], mix[span, pl.ds(0, KB * BLK)]).astype(BF)
        fsol[rows_of(i), :] = dot(uinv[rows_of(i), span], mix[span, pl.ds(KB * BLK, NR)])

    back(0)
    back(1)
    phase_wait(1)
    phase_start(2)
    wait_bytes(rsep, s_rsep)
    wait_bytes(rs_in.at[pl.ds(0, 63)], rs_recv)
    gathered = jnp.sum(rs_in[...].astype(F32), axis=0)
    xs[x * 16 + row] = (rsep[pl.ds(pl.multiple_of(row * 16, 16), 16), :].astype(F32) - gathered).astype(BF)

    def ag_body(i, carry):
        @pl.when(i != 42)
        def _():
            prow, px = peer(i)
            pltpu.make_async_remote_copy(
                src_ref=xs.at[x * 16 + row], dst_ref=xs.at[x * 16 + row], send_sem=ag_send, recv_sem=ag_recv,
                device_id=(prow, px * 2 + k), device_id_type=MESH).start()
        return carry

    lax.fori_loop(0, 64, ag_body, 0)
    for i in range(2, NT):
        back(i)
    wait_bytes(rs_in.at[pl.ds(0, 63)], ag_recv)
    phase_wait(2)

    def part_forward(z4, y4):
        acc = None
        for j in range(z4 + 1):
            term = dot(slots[z4, y4, j, pl.ds(0, BLK), :], xs[pl.ds(16 * j, 16)].reshape(TB, NR))
            acc = term if acc is None else acc + term
        return acc

    for z4 in range(4):
        for b in range(2):
            pf_send[z4, pl.ds(BLK * b, BLK)] = part_forward(z4, 2 * other + b).astype(BF)
    swap_f = pltpu.make_async_remote_copy(
        src_ref=pf_send, dst_ref=pf_recv, send_sem=core_send.at[1], recv_sem=core_recv.at[1],
        device_id=partner, device_id_type=MESH)
    swap_f.start()
    held = [[part_forward(z4, 2 * k + b) for b in range(2)] for z4 in range(4)]
    swap_f.wait_recv()
    for z4 in range(4):
        for b in range(2):
            fwd_sep[z4, pl.ds(BLK * b, BLK)] = (
                held[z4][b] + pf_recv[z4, pl.ds(BLK * b, BLK)].astype(F32)).astype(BF)

    swaps = []
    for z4 in (3, 2, 1, 0):
        for y4 in range(4):
            acc = dot(slots[z4, y4, :, pl.ds(BLK, 32), :].reshape(BLK, TB), fwd_sep[z4])
            for j in range(z4 + 1, 4):
                acc = acc + dot(slots[z4, y4, j, pl.ds(0, BLK), :], fwd_sep[j])
            ps[4 * z4 + y4] = acc.astype(BF)
        swaps.append(pltpu.make_async_remote_copy(
            src_ref=ps.at[pl.ds(4 * z4, 4)], dst_ref=pr.at[pl.ds(4 * z4, 4)],
            send_sem=core_send.at[2 + z4], recv_sem=core_recv.at[2 + z4],
            device_id=partner, device_id_type=MESH))
        swaps[-1].start()
    for s in swaps:
        s.wait_recv()

    def solved(s):
        return (ps[s].astype(F32) + pr[s].astype(F32)).astype(BF)

    osep[...] = solved(row)
    out_sep = pltpu.make_async_copy(osep, osep_h, s_osep)
    out_sep.start()
    for j in range(KB):
        coupled[pl.ds(BLK * j, BLK), :] = solved(named[j])
    outs = []
    for i in range(NT):
        part = fsol[rows_of(i), :] - dot(gmat[rows_of(i), :], coupled[...])
        obuf[rows_of(i), :] = jnp.where(keep(TB * i, TB, NR), part, 0.0).astype(BF)
        outs.append(pltpu.make_async_copy(obuf.at[rows_of(i)], out_h.at[0, rows_of(i)], s_out.at[i]))
        outs[-1].start()

    swap.wait_send()
    swap_f.wait_send()
    for s in swaps:
        s.wait_send()
    wait_bytes(rs_in.at[pl.ds(0, 63)], rs_send)
    wait_bytes(rs_in.at[pl.ds(0, 63)], ag_send)
    for ph in range(3):
        phase_drain(ph)
    out_sep.wait()
    for o in outs:
        o.wait()


def shards(
    rhs_leaf, rhs_sep, leaf_sizes, off_blocks, linv_leaf, uinv_leaf, l_off, u_off, linv_sep, uinv_sep,
):
    any_spec = pl.BlockSpec(memory_space=pl.ANY)
    smem = pl.BlockSpec(memory_space=pltpu.SMEM)
    dma = pltpu.SemaphoreType.DMA
    vm = pltpu.VMEM
    return pl.pallas_call(
        kernel,
        out_shape=(
            jax.ShapeDtypeStruct((1, W, NR), BF),
            jax.ShapeDtypeStruct((BLK, NR), BF),
        ),
        in_specs=[smem, smem] + [any_spec] * 8,
        out_specs=(any_spec, any_spec),
        scratch_shapes=[
            vm((W, W), BF), vm((W, W), BF), vm((KB * BLK, W), BF), vm((W, NR), BF),
            vm((W, KB * BLK + NR), BF), vm((W, KB * BLK), BF), vm((W, NR), F32),
            vm((KB + 1, 8, 16, NR), BF), vm((4, 4, 4, SLOT, TB), BF), vm((TB, NR), BF),
            vm((4, 16, 16, NR), BF), vm((4, 16, 16, NR), BF), vm((64, 16, NR), BF),
            vm((64, 16, NR), BF), vm((64, 16, NR), BF),
            vm((4, TB, NR), BF), vm((4, TB, NR), BF), vm((4, TB, NR), BF),
            vm((16, BLK, NR), BF), vm((16, BLK, NR), BF), vm((KB * BLK, NR), BF),
            vm((W, NR), BF), vm((BLK, NR), BF),
            dma, dma((NT,)), dma((NT,)), dma((NT,)), dma, dma, dma, dma, dma((NT,)), dma,
            dma((3, 3)), dma((3, 3)), dma, dma, dma((6,)), dma((6,)), dma, dma, dma, dma,
            pltpu.SemaphoreType.REGULAR, pltpu.SemaphoreType.REGULAR,
        ],
        compiler_params=pltpu.CompilerParams(
            collective_id=0, has_side_effects=True, vmem_limit_bytes=56 * 1024 * 1024),
        name="supernodal_solve",
    )(leaf_sizes, off_blocks, rhs_leaf, rhs_sep, linv_leaf, uinv_leaf, l_off, u_off, linv_sep, uinv_sep)


def solution(mesh):
    placed = (
        P(("row", "col"), None, None),
        P("col", None),
        P(("row", "col")),
        P(("row", "col"), None),
        P(("row", "col"), None, None),
        P(("row", "col"), None, None),
        P(("row", "col"), None, None),
        P(("row", "col"), None, None),
        P("row", "col"),
        P("row", "col"),
    )
    return jax.shard_map(
        shards,
        mesh=mesh,
        in_specs=placed,
        out_specs=(P(("row", "col"), None, None), P("row", None)),
        check_vma=False,
    )
```

```python
import jax
import jax.numpy as jnp
from jax import lax
from jax.experimental import pallas as pl
from jax.experimental.pallas import tpu as pltpu
from jax.sharding import PartitionSpec as P

MESH = pl.DeviceIdType.MESH
W = 2048
NR = 128
BLK = 128
KB = 4
TB = 256
NT = W // TB
WINDOW = 3
BF = jnp.bfloat16
F32 = jnp.float32


def dot(a, b):
    return jnp.dot(a, b, preferred_element_type=F32)


def kernel(
    sizes, offs, rhs_h, rsep_h, linv_h, uinv_h, loff_h, uoff_h, lsep_h, usep_h,
    out_h, osep_h,
    linv, uinv, loff, rhs, mix, gmat, fsol, upd, rsep,
    lcol, urow, macc, mout, mrow,
    half, recv_half, pieces, rs_in, xs, part, part_in, sol, coupled, obuf, osep,
    s_rhs, s_linv, s_loff, s_uinv, s_uoff, s_own, s_rsep, s_out, s_osep,
    l_send, l_recv, u_send, u_recv, uc_sem, m_send, m_recv,
    core_send, core_recv, rs_send, rs_recv, ag_send, ag_recv,
    sem_a,
):
    row, col = lax.axis_index("row"), lax.axis_index("col")
    z, y = row // 4, row % 4
    x, k = col // 2, col % 2
    other = 1 - k
    chip = z * 16 + y * 4 + x
    size = sizes[0]
    partner = (row, x * 2 + other)

    def along_x(step):
        return (row, ((x + step) % 4) * 2 + k)

    def wait_bytes(ref, sem):
        pltpu.make_async_copy(ref, ref, sem).wait()

    def remote(src, dst, send, recv, device):
        return pltpu.make_async_remote_copy(
            src_ref=src, dst_ref=dst, send_sem=send, recv_sem=recv,
            device_id=device, device_id_type=MESH)

    def keep(start, rows, cols):
        return lax.broadcasted_iota(jnp.int32, (rows, cols), 0) + start < size

    def rows_of(i):
        return pl.ds(TB * i, TB)

    def load_front(i):
        pltpu.make_async_copy(rhs_h.at[0, rows_of(i)], rhs.at[rows_of(i)], s_rhs.at[i]).start()
        span = pl.ds(0, TB * (i + 1))
        pltpu.make_async_copy(
            linv_h.at[0, rows_of(i), span], linv.at[rows_of(i), span], s_linv.at[i]).start()
        pltpu.make_async_copy(
            loff_h.at[0, :, rows_of(i)], loff.at[:, rows_of(i)], s_loff.at[i]).start()

    for i in range(WINDOW):
        load_front(i)

    barrier = pltpu.get_barrier_semaphore()

    def greet(i, carry):
        pl.semaphore_signal(barrier, inc=1, device_id=((row + i) % 16, col), device_id_type=MESH)
        return carry

    for step in (1, 2, 3):
        pl.semaphore_signal(barrier, inc=1, device_id=along_x(step), device_id_type=MESH)
    pl.semaphore_signal(barrier, inc=1, device_id=partner, device_id_type=MESH)
    lax.fori_loop(1, 16, greet, 0)

    pltpu.make_async_copy(lsep_h, lcol.at[row], s_own.at[0]).start()
    pltpu.make_async_copy(usep_h, urow.at[k, x], s_own.at[1]).start()
    pltpu.make_async_copy(rsep_h, rsep, s_rsep).start()

    total = [None]

    def front(i):
        span = pl.ds(0, TB * (i + 1))
        wait_bytes(rhs.at[rows_of(i)], s_rhs.at[i])
        wait_bytes(linv.at[rows_of(i), span], s_linv.at[i])
        if i + WINDOW < NT:
            load_front(i + WINDOW)
        mask = keep(TB * i, TB, NR)
        rhs[rows_of(i), :] = jnp.where(mask, rhs[rows_of(i), :].astype(F32), 0.0).astype(BF)
        val = dot(linv[rows_of(i), span], rhs[span, :])
        val = jnp.where(mask, val, 0.0).astype(BF)
        mix[rows_of(i), pl.ds(KB * BLK, NR)] = val
        wait_bytes(loff.at[:, rows_of(i)], s_loff.at[i])
        term = dot(loff[:, rows_of(i)], val)
        total[0] = term if total[0] is None else total[0] + term

    for i in range(NT - 2):
        front(i)

    pl.semaphore_wait(barrier, 19)
    for step in (1, 2, 3):
        pl.semaphore_signal(sem_a, inc=1, device_id=along_x(step), device_id_type=MESH)
    wait_bytes(lcol.at[row], s_own.at[0])
    wait_bytes(urow.at[k, x], s_own.at[1])
    for step in (2, 1, 3):
        remote(urow.at[k, x], urow.at[k, x], u_send, u_recv, along_x(step)).start()
    filled = row >= 2 * col

    @pl.when(filled)
    def _():
        def body(i, carry):
            remote(lcol.at[row], lcol.at[row], l_send, l_recv.at[row], ((row + i) % 16, col)).start()
            return carry

        lax.fori_loop(1, 16, body, 0)

    for i in range(NT - 2, NT):
        front(i)
    pltpu.make_async_copy(
        uoff_h.at[0], mix.at[:, pl.ds(0, KB * BLK)], s_uoff).start()
    for i in range(NT):
        span = pl.ds(TB * i, W - TB * i)
        pltpu.make_async_copy(
            uinv_h.at[0, rows_of(i), span], uinv.at[rows_of(i), span], s_uinv.at[i]).start()

    for j in range(KB):
        upd[j] = total[0][BLK * j:BLK * (j + 1), :].reshape(8, 16, NR).astype(BF)
    upd[KB] = jnp.zeros((8, 16, NR), BF)
    named = [offs[0, j] for j in range(KB)]

    def block(s):
        at = jnp.int32(KB)
        for j in range(KB):
            at = jnp.where(named[j] == s, j, at)
        return upd[at]

    swaps = []
    for j in range(4):
        c4 = (x + 2 + j) % 4
        for b in range(2):
            half[j, pl.ds(8 * b, 8)] = block(4 * c4 + 2 * other + b)
        swaps.append(remote(half.at[j], recv_half.at[j], core_send.at[j], core_recv.at[j], partner))
        swaps[-1].start()
    pl.semaphore_wait(sem_a, 3)
    for j in range(4):
        c4 = (x + 2 + j) % 4
        swaps[j].wait_recv()
        for b in range(2):
            mine = block(4 * c4 + 2 * k + b).astype(F32)
            got = recv_half[j, pl.ds(8 * b, 8)].astype(F32)
            pieces[c4, pl.ds(8 * b, 8)] = (mine + got).astype(BF)

        def rs_body(i, carry, c4=c4):
            prow = ((z + i // 4 + 2) % 4) * 4 + (y + i + 2) % 4
            remote(pieces.at[c4, prow], rs_in.at[chip], rs_send, rs_recv, (prow, c4 * 2 + k)).start()
            return carry

        if j == 2:
            lax.fori_loop(0, 10, rs_body, 0)
            lax.fori_loop(11, 16, rs_body, 0)
            rs_in[chip] = pieces[c4, row]
        else:
            lax.fori_loop(0, 16, rs_body, 0)

    wait_bytes(urow.at[0, pl.ds(0, 3)], u_recv)
    give_u = remote(urow.at[k], urow.at[k], uc_sem.at[0], uc_sem.at[1], partner)
    give_u.start()

    wait_bytes(mix.at[:, pl.ds(0, KB * BLK)], s_uoff)
    for i in range(NT):
        val = mix[rows_of(i), pl.ds(0, KB * BLK)].astype(F32)
        mix[rows_of(i), pl.ds(0, KB * BLK)] = jnp.where(keep(TB * i, TB, KB * BLK), val, 0.0).astype(BF)

    def back(i):
        span = pl.ds(TB * i, W - TB * i)
        wait_bytes(uinv.at[rows_of(i), span], s_uinv.at[i])
        gmat[rows_of(i), :] = dot(uinv[rows_of(i), span], mix[span, pl.ds(0, KB * BLK)]).astype(BF)
        fsol[rows_of(i), :] = dot(uinv[rows_of(i), span], mix[span, pl.ds(KB * BLK, NR)])

    back(0)
    give_u.wait_recv()

    def l_wait(i, carry):
        @pl.when(i != row)
        def _():
            wait_bytes(lcol.at[i], l_recv.at[i])
        return carry

    lax.fori_loop(2 * col, 16, l_wait, 0)
    macc[...] = jnp.zeros_like(macc)

    def m_body(c, carry):
        macc[...] += dot(urow[c % 2, c // 2], lcol[pl.ds(2 * c, 2)].reshape(TB, TB))
        return carry

    lax.fori_loop(jnp.maximum(col, row // 2), 8, m_body, 0)
    mout[...] = macc[...].reshape(4, 32, TB).astype(BF)
    for step in (2, 1, 3):
        px = (x + step) % 4
        remote(mout.at[px], mrow.at[x], m_send, m_recv, along_x(step)).start()
    mrow[x] = mout[x]
    back(1)

    wait_bytes(rsep, s_rsep)
    wait_bytes(rs_in.at[pl.ds(0, 63)], rs_recv)
    gathered = jnp.sum(rs_in[...].astype(F32), axis=0)
    xs[x * 16 + row] = (rsep[pl.ds(pl.multiple_of(row * 16, 16), 16), :].astype(F32) - gathered).astype(BF)

    def spread(ref, sem):
        def body(i, carry):
            pz, py, px = (z + i // 16 + 2) % 4, (y + i // 4 + 2) % 4, (x + i + 2) % 4
            remote(ref, ref, ag_send.at[sem], ag_recv.at[sem], (pz * 4 + py, px * 2 + k)).start()
            return carry

        lax.fori_loop(0, 42, body, 0)
        lax.fori_loop(43, 64, body, 0)

    spread(xs.at[x * 16 + row], 0)
    for i in range(2, 5):
        back(i)
    wait_bytes(mrow.at[pl.ds(0, 3)], m_recv)
    wait_bytes(rs_in.at[pl.ds(0, 63)], ag_recv.at[0])

    val = None
    for j in range(4):
        term = dot(mrow[j], xs[pl.ds(16 * j, 16)].reshape(TB, NR))
        val = term if val is None else val + term
    part[...] = val.reshape(2, 16, NR)
    swap_m = remote(part.at[other], part_in, core_send.at[4], core_recv.at[4], partner)
    swap_m.start()
    swap_m.wait_recv()
    sol[k, row, x] = (part[k] + part_in[...]).astype(BF)
    spread(sol.at[k, row, x], 1)
    for i in range(5, NT):
        back(i)
    wait_bytes(rs_in.at[pl.ds(0, 63)], ag_recv.at[1])
    swap_s = remote(sol.at[k], sol.at[k], core_send.at[5], core_recv.at[5], partner)
    swap_s.start()
    swap_s.wait_recv()

    for j in range(KB):
        for h in range(2):
            got = sol[h, named[j]]
            for q in range(4):
                coupled[pl.ds(BLK * j + 32 * q + 16 * h, 16), :] = got[q]
    outs = []
    for i in range(NT):
        val = fsol[rows_of(i), :] - dot(gmat[rows_of(i), :], coupled[...])
        obuf[rows_of(i), :] = jnp.where(keep(TB * i, TB, NR), val, 0.0).astype(BF)
        outs.append(pltpu.make_async_copy(obuf.at[rows_of(i)], out_h.at[0, rows_of(i)], s_out.at[i]))
        outs[-1].start()
    for h in range(2):
        got = sol[h, row]
        for q in range(4):
            osep[pl.ds(32 * q + 16 * h, 16), :] = got[q]
    outs.append(pltpu.make_async_copy(osep, osep_h, s_osep))
    outs[-1].start()

    for s in swaps + [swap_m, swap_s, give_u]:
        s.wait_send()
    wait_bytes(urow.at[0, pl.ds(0, 3)], u_send)
    wait_bytes(mrow.at[pl.ds(0, 3)], m_send)

    @pl.when(filled)
    def _():
        wait_bytes(lcol.at[pl.ds(0, 15)], l_send)

    for sem in (rs_send, ag_send.at[0], ag_send.at[1]):
        wait_bytes(rs_in.at[pl.ds(0, 63)], sem)
    for o in outs:
        o.wait()


def hand_over(leaf, sep, leaf_out, sep_out, sems):
    one = pltpu.make_async_copy(leaf, leaf_out, sems.at[0])
    two = pltpu.make_async_copy(sep, sep_out, sems.at[1])
    one.start()
    two.start()
    one.wait()
    two.wait()


def shards(
    rhs_leaf, rhs_sep, leaf_sizes, off_blocks, linv_leaf, uinv_leaf, l_off, u_off, linv_sep, uinv_sep,
):
    any_spec = pl.BlockSpec(memory_space=pl.ANY)
    smem = pl.BlockSpec(memory_space=pltpu.SMEM)
    dma = pltpu.SemaphoreType.DMA
    vm = pltpu.VMEM
    out_shape = (
        jax.ShapeDtypeStruct((1, W, NR), BF),
        jax.ShapeDtypeStruct((BLK, NR), BF),
    )
    solved = pl.pallas_call(
        kernel,
        out_shape=out_shape,
        in_specs=[smem, smem] + [any_spec] * 8,
        out_specs=(any_spec, any_spec),
        scratch_shapes=[
            vm((W, W), BF), vm((W, W), BF), vm((KB * BLK, W), BF), vm((W, NR), BF),
            vm((W, KB * BLK + NR), BF), vm((W, KB * BLK), BF), vm((W, NR), F32),
            vm((KB + 1, 8, 16, NR), BF), vm((TB, NR), BF),
            vm((16, BLK, TB), BF), vm((2, 4, BLK, TB), BF), vm((BLK, TB), F32),
            vm((4, 32, TB), BF), vm((4, 32, TB), BF),
            vm((4, 16, 16, NR), BF), vm((4, 16, 16, NR), BF), vm((4, 16, 16, NR), BF),
            vm((64, 16, NR), BF), vm((64, 16, NR), BF),
            vm((2, 16, NR), F32), vm((16, NR), F32), vm((2, 16, 4, 16, NR), BF),
            vm((KB * BLK, NR), BF), vm((W, NR), BF), vm((BLK, NR), BF),
            dma((NT,)), dma((NT,)), dma((NT,)), dma((NT,)), dma, dma((2,)), dma, dma((NT,)), dma,
            dma, dma((16,)), dma, dma, dma((2,)), dma, dma,
            dma((6,)), dma((6,)), dma, dma, dma((2,)), dma((2,)),
            pltpu.SemaphoreType.REGULAR,
        ],
        compiler_params=pltpu.CompilerParams(
            collective_id=0, has_side_effects=True, vmem_limit_bytes=56 * 1024 * 1024),
        name="supernodal_solve",
    )(leaf_sizes, off_blocks, rhs_leaf, rhs_sep, linv_leaf, uinv_leaf, l_off, u_off, linv_sep, uinv_sep)
    return pl.pallas_call(
        hand_over,
        out_shape=out_shape,
        in_specs=[any_spec, any_spec],
        out_specs=(any_spec, any_spec),
        scratch_shapes=[dma((2,))],
        compiler_params=pltpu.CompilerParams(vmem_limit_bytes=56 * 1024 * 1024),
        name="hand_over",
    )(*solved)


def solution(mesh):
    placed = (
        P(("row", "col"), None, None),
        P("col", None),
        P(("row", "col")),
        P(("row", "col"), None),
        P(("row", "col"), None, None),
        P(("row", "col"), None, None),
        P(("row", "col"), None, None),
        P(("row", "col"), None, None),
        P("row", "col"),
        P("row", "col"),
    )
    return jax.shard_map(
        shards,
        mesh=mesh,
        in_specs=placed,
        out_specs=(P(("row", "col"), None, None), P("row", None)),
        check_vma=False,
    )
```

```python
import jax
import jax.numpy as jnp
from jax import lax
from jax.experimental import pallas as pl
from jax.experimental.pallas import tpu as pltpu
from jax.sharding import PartitionSpec as P

MESH = pl.DeviceIdType.MESH
W = 2048
NR = 128
BLK = 128
KB = 4
TB = 256
NT = W // TB
WINDOW = 3
BF = jnp.bfloat16
F32 = jnp.float32


def dot(a, b):
    return jnp.dot(a, b, preferred_element_type=F32)


def kernel(
    sizes, offs, rhs_h, rsep_h, linv_h, uinv_h, loff_h, uoff_h, lsep_h, usep_h,
    out, osep,
    linv, uinv, loff, rhs, mix, gmat, fsol, upd, rsep,
    lcol, urow, macc, mout, mrow,
    half, recv_half, pieces, rs_in, xs, part, part_in, sol, coupled,
    s_rhs, s_linv, s_loff, s_uinv, s_uoff, s_own, s_rsep,
    l_send, l_recv, u_send, u_recv, uc_sem, m_send, m_recv,
    core_send, core_recv, rs_send, rs_recv, ag_send, ag_recv,
    sem_a,
):
    row, col = lax.axis_index("row"), lax.axis_index("col")
    z, y = row // 4, row % 4
    x, k = col // 2, col % 2
    other = 1 - k
    chip = z * 16 + y * 4 + x
    size = sizes[0]
    partner = (row, x * 2 + other)

    def along_x(step):
        return (row, ((x + step) % 4) * 2 + k)

    def wait_bytes(ref, sem):
        pltpu.make_async_copy(ref, ref, sem).wait()

    def remote(src, dst, send, recv, device):
        return pltpu.make_async_remote_copy(
            src_ref=src, dst_ref=dst, send_sem=send, recv_sem=recv,
            device_id=device, device_id_type=MESH)

    def keep(start, rows, cols):
        return lax.broadcasted_iota(jnp.int32, (rows, cols), 0) + start < size

    def rows_of(i):
        return pl.ds(TB * i, TB)

    def load_front(i):
        pltpu.make_async_copy(rhs_h.at[0, rows_of(i)], rhs.at[rows_of(i)], s_rhs.at[i]).start()
        span = pl.ds(0, TB * (i + 1))
        pltpu.make_async_copy(
            linv_h.at[0, rows_of(i), span], linv.at[rows_of(i), span], s_linv.at[i]).start()
        pltpu.make_async_copy(
            loff_h.at[0, :, rows_of(i)], loff.at[:, rows_of(i)], s_loff.at[i]).start()

    for i in range(WINDOW):
        load_front(i)

    barrier = pltpu.get_barrier_semaphore()

    def greet(i, carry):
        pl.semaphore_signal(barrier, inc=1, device_id=((row + i) % 16, col), device_id_type=MESH)
        return carry

    for step in (1, 2, 3):
        pl.semaphore_signal(barrier, inc=1, device_id=along_x(step), device_id_type=MESH)
    pl.semaphore_signal(barrier, inc=1, device_id=partner, device_id_type=MESH)
    lax.fori_loop(1, 16, greet, 0)

    pltpu.make_async_copy(lsep_h, lcol.at[row], s_own.at[0]).start()
    pltpu.make_async_copy(usep_h, urow.at[k, x], s_own.at[1]).start()
    pltpu.make_async_copy(rsep_h, rsep, s_rsep).start()

    total = [None]

    def front(i):
        span = pl.ds(0, TB * (i + 1))
        wait_bytes(rhs.at[rows_of(i)], s_rhs.at[i])
        wait_bytes(linv.at[rows_of(i), span], s_linv.at[i])
        if i + WINDOW < NT:
            load_front(i + WINDOW)
        mask = keep(TB * i, TB, NR)
        rhs[rows_of(i), :] = jnp.where(mask, rhs[rows_of(i), :].astype(F32), 0.0).astype(BF)
        val = dot(linv[rows_of(i), span], rhs[span, :])
        val = jnp.where(mask, val, 0.0).astype(BF)
        mix[rows_of(i), pl.ds(KB * BLK, NR)] = val
        wait_bytes(loff.at[:, rows_of(i)], s_loff.at[i])
        term = dot(loff[:, rows_of(i)], val)
        total[0] = term if total[0] is None else total[0] + term

    for i in range(NT - 3):
        front(i)

    pl.semaphore_wait(barrier, 19)
    for step in (1, 2, 3):
        pl.semaphore_signal(sem_a, inc=1, device_id=along_x(step), device_id_type=MESH)
    wait_bytes(lcol.at[row], s_own.at[0])
    wait_bytes(urow.at[k, x], s_own.at[1])
    for step in (2, 1, 3):
        remote(urow.at[k, x], urow.at[k, x], u_send, u_recv, along_x(step)).start()
    filled = row >= 2 * col

    @pl.when(filled)
    def _():
        def body(i, carry):
            remote(lcol.at[row], lcol.at[row], l_send, l_recv.at[row], ((row + i) % 16, col)).start()
            return carry

        lax.fori_loop(1, 16, body, 0)

    for i in range(NT - 3, NT):
        front(i)
    pltpu.make_async_copy(
        uoff_h.at[0], mix.at[:, pl.ds(0, KB * BLK)], s_uoff).start()
    for i in range(NT):
        span = pl.ds(TB * i, W - TB * i)
        pltpu.make_async_copy(
            uinv_h.at[0, rows_of(i), span], uinv.at[rows_of(i), span], s_uinv.at[i]).start()

    for j in range(KB):
        upd[j] = total[0][BLK * j:BLK * (j + 1), :].reshape(8, 16, NR).astype(BF)
    upd[KB] = jnp.zeros((8, 16, NR), BF)
    named = [offs[0, j] for j in range(KB)]

    def block(s):
        at = jnp.int32(KB)
        for j in range(KB):
            at = jnp.where(named[j] == s, j, at)
        return upd[at]

    swaps = []
    for j in range(4):
        c4 = (x + 2 + j) % 4
        for b in range(2):
            half[j, pl.ds(8 * b, 8)] = block(4 * c4 + 2 * other + b)
        swaps.append(remote(half.at[j], recv_half.at[j], core_send.at[j], core_recv.at[j], partner))
        swaps[-1].start()
    pl.semaphore_wait(sem_a, 3)
    for j in range(4):
        c4 = (x + 2 + j) % 4
        swaps[j].wait_recv()
        for b in range(2):
            mine = block(4 * c4 + 2 * k + b).astype(F32)
            got = recv_half[j, pl.ds(8 * b, 8)].astype(F32)
            pieces[c4, pl.ds(8 * b, 8)] = (mine + got).astype(BF)

        def rs_body(i, carry, c4=c4):
            prow = ((z + i // 4 + 2) % 4) * 4 + (y + i + 2) % 4
            remote(pieces.at[c4, prow], rs_in.at[chip], rs_send, rs_recv, (prow, c4 * 2 + k)).start()
            return carry

        if j == 2:
            lax.fori_loop(0, 10, rs_body, 0)
            lax.fori_loop(11, 16, rs_body, 0)
            rs_in[chip] = pieces[c4, row]
        else:
            lax.fori_loop(0, 16, rs_body, 0)

    wait_bytes(urow.at[0, pl.ds(0, 3)], u_recv)
    give_u = remote(urow.at[k], urow.at[k], uc_sem.at[0], uc_sem.at[1], partner)
    give_u.start()

    wait_bytes(mix.at[:, pl.ds(0, KB * BLK)], s_uoff)
    for i in range(NT):
        val = mix[rows_of(i), pl.ds(0, KB * BLK)].astype(F32)
        mix[rows_of(i), pl.ds(0, KB * BLK)] = jnp.where(keep(TB * i, TB, KB * BLK), val, 0.0).astype(BF)

    def back(i):
        span = pl.ds(TB * i, W - TB * i)
        wait_bytes(uinv.at[rows_of(i), span], s_uinv.at[i])
        gmat[rows_of(i), :] = dot(uinv[rows_of(i), span], mix[span, pl.ds(0, KB * BLK)]).astype(BF)
        fsol[rows_of(i), :] = dot(uinv[rows_of(i), span], mix[span, pl.ds(KB * BLK, NR)])

    back(0)
    back(1)

    wait_bytes(rsep, s_rsep)
    wait_bytes(rs_in.at[pl.ds(0, 63)], rs_recv)
    gathered = jnp.sum(rs_in[...].astype(F32), axis=0)
    xs[x * 16 + row] = (rsep[pl.ds(pl.multiple_of(row * 16, 16), 16), :].astype(F32) - gathered).astype(BF)

    def spread(ref, sem):
        def body(i, carry):
            pz, py, px = (z + i // 16 + 2) % 4, (y + i // 4 + 2) % 4, (x + i + 2) % 4
            remote(ref, ref, ag_send.at[sem], ag_recv.at[sem], (pz * 4 + py, px * 2 + k)).start()
            return carry

        lax.fori_loop(0, 42, body, 0)
        lax.fori_loop(43, 64, body, 0)

    spread(xs.at[x * 16 + row], 0)
    give_u.wait_recv()

    def l_wait(i, carry):
        @pl.when(i != row)
        def _():
            wait_bytes(lcol.at[i], l_recv.at[i])
        return carry

    lax.fori_loop(2 * col, 16, l_wait, 0)
    macc[...] = jnp.zeros_like(macc)

    def m_body(c, carry):
        macc[...] += dot(urow[c % 2, c // 2], lcol[pl.ds(2 * c, 2)].reshape(TB, TB))
        return carry

    lax.fori_loop(jnp.maximum(col, row // 2), 8, m_body, 0)
    mout[...] = macc[...].reshape(4, 32, TB).astype(BF)
    for step in (2, 1, 3):
        px = (x + step) % 4
        remote(mout.at[px], mrow.at[x], m_send, m_recv, along_x(step)).start()
    mrow[x] = mout[x]
    for i in range(2, 5):
        back(i)
    wait_bytes(mrow.at[pl.ds(0, 3)], m_recv)
    wait_bytes(rs_in.at[pl.ds(0, 63)], ag_recv.at[0])

    val = None
    for j in range(4):
        term = dot(mrow[j], xs[pl.ds(16 * j, 16)].reshape(TB, NR))
        val = term if val is None else val + term
    part[...] = val.reshape(2, 16, NR)
    swap_m = remote(part.at[other], part_in, core_send.at[4], core_recv.at[4], partner)
    swap_m.start()
    swap_m.wait_recv()
    sol[k, row, x] = (part[k] + part_in[...]).astype(BF)
    spread(sol.at[k, row, x], 1)
    for i in range(5, NT):
        back(i)
    wait_bytes(rs_in.at[pl.ds(0, 63)], ag_recv.at[1])
    swap_s = remote(sol.at[k], sol.at[k], core_send.at[5], core_recv.at[5], partner)
    swap_s.start()
    swap_s.wait_recv()

    for j in range(KB):
        for h in range(2):
            got = sol[h, named[j]]
            for q in range(4):
                coupled[pl.ds(BLK * j + 32 * q + 16 * h, 16), :] = got[q]
    for i in range(NT):
        val = fsol[rows_of(i), :] - dot(gmat[rows_of(i), :], coupled[...])
        out[0, rows_of(i), :] = jnp.where(keep(TB * i, TB, NR), val, 0.0).astype(BF)
    for h in range(2):
        got = sol[h, row]
        for q in range(4):
            osep[pl.ds(32 * q + 16 * h, 16), :] = got[q]

    for s in swaps + [swap_m, swap_s, give_u]:
        s.wait_send()
    wait_bytes(urow.at[0, pl.ds(0, 3)], u_send)
    wait_bytes(mrow.at[pl.ds(0, 3)], m_send)

    @pl.when(filled)
    def _():
        wait_bytes(lcol.at[pl.ds(0, 15)], l_send)

    for sem in (rs_send, ag_send.at[0], ag_send.at[1]):
        wait_bytes(rs_in.at[pl.ds(0, 63)], sem)


def hand_over(leaf, sep, leaf_out, sep_out, sems):
    one = pltpu.make_async_copy(leaf, leaf_out, sems.at[0])
    two = pltpu.make_async_copy(sep, sep_out, sems.at[1])
    one.start()
    two.start()
    one.wait()
    two.wait()


def shards(
    rhs_leaf, rhs_sep, leaf_sizes, off_blocks, linv_leaf, uinv_leaf, l_off, u_off, linv_sep, uinv_sep,
):
    any_spec = pl.BlockSpec(memory_space=pl.ANY)
    smem = pl.BlockSpec(memory_space=pltpu.SMEM)
    dma = pltpu.SemaphoreType.DMA
    vm = pltpu.VMEM
    solved = pl.pallas_call(
        kernel,
        out_shape=(vm((1, W, NR), BF), vm((BLK, NR), BF)),
        in_specs=[smem, smem] + [any_spec] * 8,
        out_specs=(pl.BlockSpec(memory_space=vm), pl.BlockSpec(memory_space=vm)),
        scratch_shapes=[
            vm((W, W), BF), vm((W, W), BF), vm((KB * BLK, W), BF), vm((W, NR), BF),
            vm((W, KB * BLK + NR), BF), vm((W, KB * BLK), BF), vm((W, NR), F32),
            vm((KB + 1, 8, 16, NR), BF), vm((TB, NR), BF),
            vm((16, BLK, TB), BF), vm((2, 4, BLK, TB), BF), vm((BLK, TB), F32),
            vm((4, 32, TB), BF), vm((4, 32, TB), BF),
            vm((4, 16, 16, NR), BF), vm((4, 16, 16, NR), BF), vm((4, 16, 16, NR), BF),
            vm((64, 16, NR), BF), vm((64, 16, NR), BF),
            vm((2, 16, NR), F32), vm((16, NR), F32), vm((2, 16, 4, 16, NR), BF),
            vm((KB * BLK, NR), BF),
            dma((NT,)), dma((NT,)), dma((NT,)), dma((NT,)), dma, dma((2,)), dma,
            dma, dma((16,)), dma, dma, dma((2,)), dma, dma,
            dma((6,)), dma((6,)), dma, dma, dma((2,)), dma((2,)),
            pltpu.SemaphoreType.REGULAR,
        ],
        compiler_params=pltpu.CompilerParams(
            collective_id=0, has_side_effects=True, vmem_limit_bytes=56 * 1024 * 1024),
        name="supernodal_solve",
    )(leaf_sizes, off_blocks, rhs_leaf, rhs_sep, linv_leaf, uinv_leaf, l_off, u_off, linv_sep, uinv_sep)
    return pl.pallas_call(
        hand_over,
        out_shape=(jax.ShapeDtypeStruct((1, W, NR), BF), jax.ShapeDtypeStruct((BLK, NR), BF)),
        in_specs=[pl.BlockSpec(memory_space=vm), pl.BlockSpec(memory_space=vm)],
        out_specs=(any_spec, any_spec),
        scratch_shapes=[dma((2,))],
        compiler_params=pltpu.CompilerParams(vmem_limit_bytes=4 * 1024 * 1024),
        name="hand_over",
    )(*solved)


def solution(mesh):
    placed = (
        P(("row", "col"), None, None),
        P("col", None),
        P(("row", "col")),
        P(("row", "col"), None),
        P(("row", "col"), None, None),
        P(("row", "col"), None, None),
        P(("row", "col"), None, None),
        P(("row", "col"), None, None),
        P("row", "col"),
        P("row", "col"),
    )
    return jax.shard_map(
        shards,
        mesh=mesh,
        in_specs=placed,
        out_specs=(P(("row", "col"), None, None), P("row", None)),
        check_vma=False,
    )
```

```python
import jax
import jax.numpy as jnp
from jax import lax
from jax.experimental import pallas as pl
from jax.experimental.pallas import tpu as pltpu
from jax.sharding import PartitionSpec as P

MESH = pl.DeviceIdType.MESH
W = 2048
NR = 128
BLK = 128
KB = 4
TB = 256
NT = W // TB
WINDOW = 3
BF = jnp.bfloat16
F32 = jnp.float32


def dot(a, b):
    return jnp.dot(a, b, preferred_element_type=F32)


def kernel(
    sizes, offs, rhs_h, rsep_h, linv_h, uinv_h, loff_h, uoff_h, lsep_h, usep_h,
    out, osep,
    linv, uinv, loff, rhs, mix, gmat, fsol, upd, rsep,
    lcol, urow, macc, mout, mrow,
    half, recv_half, pieces, rs_in, xs, part, part_in, sol, coupled,
    s_rhs, s_linv, s_loff, s_uinv, s_uoff, s_own, s_rsep,
    l_send, l_recv, n_send, n_recv, f_send, f_recv, u_send, u_recv, uc_sem, m_send, m_recv,
    core_send, core_recv, rs_send, rs_recv, ag_send, ag_recv, sol_recv,
    sem_a,
):
    row, col = lax.axis_index("row"), lax.axis_index("col")
    z, y = row // 4, row % 4
    x, k = col // 2, col % 2
    other = 1 - k
    chip = z * 16 + y * 4 + x
    size = sizes[0]
    partner = (row, x * 2 + other)

    def along_x(step):
        return (row, ((x + step) % 4) * 2 + k)

    def along(cl, step):
        if cl == 0:
            return (z * 4 + (y + step) % 4, col)
        return (((z + step) % 4) * 4 + y, col)

    def wait_bytes(ref, sem):
        pltpu.make_async_copy(ref, ref, sem).wait()

    def remote(src, dst, send, recv, device):
        return pltpu.make_async_remote_copy(
            src_ref=src, dst_ref=dst, send_sem=send, recv_sem=recv,
            device_id=device, device_id_type=MESH)

    def keep(start, rows, cols):
        return lax.broadcasted_iota(jnp.int32, (rows, cols), 0) + start < size

    def rows_of(i):
        return pl.ds(TB * i, TB)

    def load_front(i):
        pltpu.make_async_copy(rhs_h.at[0, rows_of(i)], rhs.at[rows_of(i)], s_rhs.at[i]).start()
        span = pl.ds(0, TB * (i + 1))
        pltpu.make_async_copy(
            linv_h.at[0, rows_of(i), span], linv.at[rows_of(i), span], s_linv.at[i]).start()
        pltpu.make_async_copy(
            loff_h.at[0, :, rows_of(i)], loff.at[:, rows_of(i)], s_loff.at[i]).start()

    for i in range(WINDOW):
        load_front(i)

    barrier = pltpu.get_barrier_semaphore()

    def greet(i, carry):
        pl.semaphore_signal(barrier, inc=1, device_id=((row + i) % 16, col), device_id_type=MESH)
        return carry

    for step in (1, 2, 3):
        pl.semaphore_signal(barrier, inc=1, device_id=along_x(step), device_id_type=MESH)
    pl.semaphore_signal(barrier, inc=1, device_id=partner, device_id_type=MESH)
    lax.fori_loop(1, 16, greet, 0)

    pltpu.make_async_copy(lsep_h, lcol.at[z, y], s_own.at[0]).start()
    pltpu.make_async_copy(usep_h, urow.at[k, x], s_own.at[1]).start()
    pltpu.make_async_copy(rsep_h, rsep, s_rsep).start()

    total = [None]

    def front(i):
        span = pl.ds(0, TB * (i + 1))
        wait_bytes(rhs.at[rows_of(i)], s_rhs.at[i])
        wait_bytes(linv.at[rows_of(i), span], s_linv.at[i])
        if i + WINDOW < NT:
            load_front(i + WINDOW)
        mask = keep(TB * i, TB, NR)
        rhs[rows_of(i), :] = jnp.where(mask, rhs[rows_of(i), :].astype(F32), 0.0).astype(BF)
        val = dot(linv[rows_of(i), span], rhs[span, :])
        val = jnp.where(mask, val, 0.0).astype(BF)
        mix[rows_of(i), pl.ds(KB * BLK, NR)] = val
        wait_bytes(loff.at[:, rows_of(i)], s_loff.at[i])
        term = dot(loff[:, rows_of(i)], val)
        total[0] = term if total[0] is None else total[0] + term

    for i in range(NT - 1):
        front(i)

    pl.semaphore_wait(barrier, 19)
    for step in (1, 2, 3):
        pl.semaphore_signal(sem_a, inc=1, device_id=along_x(step), device_id_type=MESH)
    wait_bytes(lcol.at[z, y], s_own.at[0])
    wait_bytes(urow.at[k, x], s_own.at[1])
    for step in (2, 1, 3):
        for cl in range(2):
            ref = lcol.at[z, y, pl.ds(64 * cl, 64)]
            remote(ref, ref, l_send.at[cl], l_recv.at[cl], along(cl, step)).start()
        remote(urow.at[k, x], urow.at[k, x], u_send, u_recv, along_x(step)).start()

    front(NT - 1)
    pltpu.make_async_copy(
        uoff_h.at[0], mix.at[:, pl.ds(0, KB * BLK)], s_uoff).start()
    for i in range(NT):
        span = pl.ds(TB * i, W - TB * i)
        pltpu.make_async_copy(
            uinv_h.at[0, rows_of(i), span], uinv.at[rows_of(i), span], s_uinv.at[i]).start()

    for j in range(KB):
        upd[j] = total[0][BLK * j:BLK * (j + 1), :].reshape(8, 16, NR).astype(BF)
    upd[KB] = jnp.zeros((8, 16, NR), BF)
    named = [offs[0, j] for j in range(KB)]

    def block(s):
        at = jnp.int32(KB)
        for j in range(KB):
            at = jnp.where(named[j] == s, j, at)
        return upd[at]

    swaps = []
    for j in range(4):
        c4 = (x + 2 + j) % 4
        for b in range(2):
            half[j, pl.ds(8 * b, 8)] = block(4 * c4 + 2 * other + b)
        swaps.append(remote(half.at[j], recv_half.at[j], core_send.at[j], core_recv.at[j], partner))
        swaps[-1].start()
    pl.semaphore_wait(sem_a, 3)
    for j in range(4):
        c4 = (x + 2 + j) % 4
        swaps[j].wait_recv()
        for b in range(2):
            mine = block(4 * c4 + 2 * k + b).astype(F32)
            got = recv_half[j, pl.ds(8 * b, 8)].astype(F32)
            pieces[c4, pl.ds(8 * b, 8)] = (mine + got).astype(BF)

        def rs_body(i, carry, c4=c4):
            prow = ((z + i // 4 + 2) % 4) * 4 + (y + i + 2) % 4
            remote(pieces.at[c4, prow], rs_in.at[chip], rs_send, rs_recv, (prow, c4 * 2 + k)).start()
            return carry

        if j == 2:
            lax.fori_loop(0, 10, rs_body, 0)
            lax.fori_loop(11, 16, rs_body, 0)
            rs_in[chip] = pieces[c4, row]
        else:
            lax.fori_loop(0, 16, rs_body, 0)

    def unit(cl, at, h):
        if cl == 0:
            return lcol.at[at, pl.ds(2 * h, 2), pl.ds(0, 64)]
        return lcol.at[pl.ds(2 * h, 2), at, pl.ds(64, 64)]

    def place(cl, step):
        return ((z if cl == 0 else y) + step) % 4

    for cl in range(2):
        wait_bytes(lcol.at[0, pl.ds(0, 3), pl.ds(0, 64)], l_recv.at[cl])
    for d, h in ((0, 0), (1, 1), (0, 1), (1, 0)):
        for cl in range(2):
            ref = unit(cl, place(cl, 0), h)
            remote(ref, ref, n_send.at[cl, d, h], n_recv.at[cl, d, h], along(1 - cl, 1 + 2 * d)).start()

    wait_bytes(urow.at[0, pl.ds(0, 3)], u_recv)
    give_u = remote(urow.at[k], urow.at[k], uc_sem.at[0], uc_sem.at[1], partner)
    give_u.start()

    wait_bytes(mix.at[:, pl.ds(0, KB * BLK)], s_uoff)
    for i in range(NT):
        val = mix[rows_of(i), pl.ds(0, KB * BLK)].astype(F32)
        mix[rows_of(i), pl.ds(0, KB * BLK)] = jnp.where(keep(TB * i, TB, KB * BLK), val, 0.0).astype(BF)

    def back(i):
        span = pl.ds(TB * i, W - TB * i)
        wait_bytes(uinv.at[rows_of(i), span], s_uinv.at[i])
        gmat[rows_of(i), :] = dot(uinv[rows_of(i), span], mix[span, pl.ds(0, KB * BLK)]).astype(BF)
        fsol[rows_of(i), :] = dot(uinv[rows_of(i), span], mix[span, pl.ds(KB * BLK, NR)])

    back(0)
    back(1)
    for d in range(2):
        for cl in range(2):
            ref = unit(cl, place(cl, 3 - 2 * d), d)
            wait_bytes(ref, n_recv.at[cl, d, d])
            remote(ref, ref, f_send.at[cl, d], f_recv.at[cl, d], along(1 - cl, 1 + 2 * d)).start()

    wait_bytes(rsep, s_rsep)
    wait_bytes(rs_in.at[pl.ds(0, 63)], rs_recv)
    gathered = jnp.sum(rs_in[...].astype(F32), axis=0)
    xs[x * 16 + row] = (rsep[pl.ds(pl.multiple_of(row * 16, 16), 16), :].astype(F32) - gathered).astype(BF)

    def spread(ref, send, recv):
        def body(i, carry):
            pz, py, px = (z + i // 16 + 2) % 4, (y + i // 4 + 2) % 4, (x + i + 2) % 4
            remote(ref, ref, send, recv, (pz * 4 + py, px * 2 + k)).start()
            return carry

        lax.fori_loop(0, 42, body, 0)
        lax.fori_loop(43, 64, body, 0)

    spread(xs.at[x * 16 + row], ag_send.at[0], ag_recv)
    give_u.wait_recv()

    for d in range(2):
        for cl in range(2):
            wait_bytes(unit(cl, 0, 1 - d), n_recv.at[cl, d, 1 - d])
            wait_bytes(unit(cl, 0, d), f_recv.at[cl, d])
    macc[...] = jnp.zeros_like(macc)

    def m_body(c, carry):
        macc[...] += dot(urow[c % 2, c // 2], lcol[c // 2, pl.ds(2 * (c % 2), 2)].reshape(TB, TB))
        return carry

    lax.fori_loop(jnp.maximum(col, row // 2), 8, m_body, 0)
    mout[...] = macc[...].reshape(4, 32, TB).astype(BF)
    for step in (2, 1, 3):
        px = (x + step) % 4
        remote(mout.at[px], mrow.at[x], m_send, m_recv, along_x(step)).start()
    mrow[x] = mout[x]
    for i in range(2, 5):
        back(i)
    wait_bytes(mrow.at[pl.ds(0, 3)], m_recv)
    wait_bytes(rs_in.at[pl.ds(0, 63)], ag_recv)

    val = None
    for j in range(4):
        term = dot(mrow[j], xs[pl.ds(16 * j, 16)].reshape(TB, NR))
        val = term if val is None else val + term
    part[...] = val.reshape(2, 16, NR)
    swap_m = remote(part.at[other], part_in, core_send.at[4], core_recv.at[4], partner)
    swap_m.start()
    swap_m.wait_recv()
    sol[k, row, x] = (part[k] + part_in[...]).astype(BF)
    spread(sol.at[k, row, x], ag_send.at[1], sol_recv.at[z])
    for i in range(5, NT):
        back(i)
    last = []
    for step in (0, 1, 3, 2):
        pz = (z + step) % 4
        wait_bytes(rs_in.at[pl.ds(0, 16 if step else 15)], sol_recv.at[pz])
        ref = sol.at[k, pl.ds(4 * pz, 4)]
        last.append(remote(ref, ref, core_send.at[5 + step], core_recv.at[5 + step], partner))
        last[-1].start()
    for r in last:
        r.wait_recv()

    for j in range(KB):
        for h in range(2):
            got = sol[h, named[j]]
            for q in range(4):
                coupled[pl.ds(BLK * j + 32 * q + 16 * h, 16), :] = got[q]
    for i in range(NT):
        val = fsol[rows_of(i), :] - dot(gmat[rows_of(i), :], coupled[...])
        out[0, rows_of(i), :] = jnp.where(keep(TB * i, TB, NR), val, 0.0).astype(BF)
    for h in range(2):
        got = sol[h, row]
        for q in range(4):
            osep[pl.ds(32 * q + 16 * h, 16), :] = got[q]

    for s in swaps + last + [swap_m, give_u]:
        s.wait_send()
    wait_bytes(urow.at[0, pl.ds(0, 3)], u_send)
    wait_bytes(mrow.at[pl.ds(0, 3)], m_send)

    for cl in range(2):
        wait_bytes(lcol.at[0, pl.ds(0, 3), pl.ds(0, 64)], l_send.at[cl])
        for d in range(2):
            wait_bytes(unit(cl, 0, d), f_send.at[cl, d])
            for h in range(2):
                wait_bytes(unit(cl, 0, h), n_send.at[cl, d, h])
    for sem in (rs_send, ag_send.at[0], ag_send.at[1]):
        wait_bytes(rs_in.at[pl.ds(0, 63)], sem)


def hand_over(leaf, sep, leaf_out, sep_out, sems):
    one = pltpu.make_async_copy(leaf, leaf_out, sems.at[0])
    two = pltpu.make_async_copy(sep, sep_out, sems.at[1])
    one.start()
    two.start()
    one.wait()
    two.wait()


def shards(
    rhs_leaf, rhs_sep, leaf_sizes, off_blocks, linv_leaf, uinv_leaf, l_off, u_off, linv_sep, uinv_sep,
):
    any_spec = pl.BlockSpec(memory_space=pl.ANY)
    smem = pl.BlockSpec(memory_space=pltpu.SMEM)
    dma = pltpu.SemaphoreType.DMA
    vm = pltpu.VMEM
    solved = pl.pallas_call(
        kernel,
        out_shape=(vm((1, W, NR), BF), vm((BLK, NR), BF)),
        in_specs=[smem, smem] + [any_spec] * 8,
        out_specs=(pl.BlockSpec(memory_space=vm), pl.BlockSpec(memory_space=vm)),
        scratch_shapes=[
            vm((W, W), BF), vm((W, W), BF), vm((KB * BLK, W), BF), vm((W, NR), BF),
            vm((W, KB * BLK + NR), BF), vm((W, KB * BLK), BF), vm((W, NR), F32),
            vm((KB + 1, 8, 16, NR), BF), vm((TB, NR), BF),
            vm((4, 4, BLK, TB), BF), vm((2, 4, BLK, TB), BF), vm((BLK, TB), F32),
            vm((4, 32, TB), BF), vm((4, 32, TB), BF),
            vm((4, 16, 16, NR), BF), vm((4, 16, 16, NR), BF), vm((4, 16, 16, NR), BF),
            vm((64, 16, NR), BF), vm((64, 16, NR), BF),
            vm((2, 16, NR), F32), vm((16, NR), F32), vm((2, 16, 4, 16, NR), BF),
            vm((KB * BLK, NR), BF),
            dma((NT,)), dma((NT,)), dma((NT,)), dma((NT,)), dma, dma((2,)), dma,
            dma((2,)), dma((2,)), dma((2, 2, 2)), dma((2, 2, 2)), dma((2, 2)), dma((2, 2)),
            dma, dma, dma((2,)), dma, dma,
            dma((9,)), dma((9,)), dma, dma, dma((2,)), dma, dma((4,)),
            pltpu.SemaphoreType.REGULAR,
        ],
        compiler_params=pltpu.CompilerParams(
            collective_id=0, has_side_effects=True, vmem_limit_bytes=56 * 1024 * 1024),
        name="supernodal_solve",
    )(leaf_sizes, off_blocks, rhs_leaf, rhs_sep, linv_leaf, uinv_leaf, l_off, u_off, linv_sep, uinv_sep)
    return pl.pallas_call(
        hand_over,
        out_shape=(jax.ShapeDtypeStruct((1, W, NR), BF), jax.ShapeDtypeStruct((BLK, NR), BF)),
        in_specs=[pl.BlockSpec(memory_space=vm), pl.BlockSpec(memory_space=vm)],
        out_specs=(any_spec, any_spec),
        scratch_shapes=[dma((2,))],
        compiler_params=pltpu.CompilerParams(vmem_limit_bytes=4 * 1024 * 1024),
        name="hand_over",
    )(*solved)


def solution(mesh):
    placed = (
        P(("row", "col"), None, None),
        P("col", None),
        P(("row", "col")),
        P(("row", "col"), None),
        P(("row", "col"), None, None),
        P(("row", "col"), None, None),
        P(("row", "col"), None, None),
        P(("row", "col"), None, None),
        P("row", "col"),
        P("row", "col"),
    )
    return jax.shard_map(
        shards,
        mesh=mesh,
        in_specs=placed,
        out_specs=(P(("row", "col"), None, None), P("row", None)),
        check_vma=False,
    )
```

```python
import jax
import jax.numpy as jnp
from jax import lax
from jax.experimental import pallas as pl
from jax.experimental.pallas import tpu as pltpu
from jax.sharding import PartitionSpec as P

MESH = pl.DeviceIdType.MESH
W = 2048
NR = 128
BLK = 128
KB = 4
TB = 256
NT = W // TB
WINDOW = 4
EARLY = 4
FAR_PLANE = sorted(
    [(i // 4, i % 4) for i in range(1, 16)],
    key=lambda d: -(min(d[0], 4 - d[0]) + min(d[1], 4 - d[1])))
BF = jnp.bfloat16
F32 = jnp.float32


def dot(a, b):
    return jnp.dot(a, b, preferred_element_type=F32)


def kernel(
    sizes_h, offs_h, rhs_h, rsep_h, linv_h, uinv_h, loff_h, uoff_h, lsep_h, usep_h,
    gmat, fsol, coupled, osep,
    linv, uinv, loff, rhs, mix, upd, rsep,
    lcol, urow, macc,
    half, recv_half, pieces, rs_in, xs, part, part_in, sol,
    s_front, s_back, s_own, s_send, l_recv, u_recv, near_recv, m_recv, p_recv,
    swap_recv, last_recv, rs_recv, ag_recv, sol_recv,
    sem_a, sizes, offs, s_sizes, s_offs,
):
    row, col = lax.axis_index("row"), lax.axis_index("col")
    z, y = row // 4, row % 4
    x, k = col // 2, col % 2
    other = 1 - k
    chip = z * 16 + y * 4 + x
    partner = (row, x * 2 + other)

    def along_x(step):
        return (row, ((x + step) % 4) * 2 + k)

    def along(cl, step):
        if cl == 0:
            return (z * 4 + (y + step) % 4, col)
        return (((z + step) % 4) * 4 + y, col)

    def wait_bytes(ref, sem):
        pltpu.make_async_copy(ref, ref, sem).wait()

    def wait_kib(count, sem):
        wait_bytes(linv.at[pl.ds(0, count // 4)], sem)

    def remote(src, dst, recv, device):
        return pltpu.make_async_remote_copy(
            src_ref=src, dst_ref=dst, send_sem=s_send, recv_sem=recv,
            device_id=device, device_id_type=MESH)

    def keep(start, rows, cols):
        return lax.broadcasted_iota(jnp.int32, (rows, cols), 0) + start < sizes[0]

    def rows_of(i):
        return pl.ds(TB * i, TB)

    def load_front(i):
        pltpu.make_async_copy(rhs_h.at[0, rows_of(i)], rhs.at[rows_of(i)], s_front.at[i % WINDOW]).start()
        span = pl.ds(0, TB * (i + 1))
        pltpu.make_async_copy(
            linv_h.at[0, rows_of(i), span], linv.at[rows_of(i), span], s_front.at[i % WINDOW]).start()
        pltpu.make_async_copy(
            loff_h.at[0, :, rows_of(i)], loff.at[:, rows_of(i)], s_front.at[i % WINDOW]).start()

    pltpu.make_async_copy(sizes_h, sizes, s_sizes).start()
    for i in range(WINDOW):
        load_front(i)
    pltpu.make_async_copy(offs_h, offs, s_offs).start()

    barrier = pltpu.get_barrier_semaphore()

    def greet(i, carry):
        pl.semaphore_signal(barrier, inc=1, device_id=((row + i) % 16, col), device_id_type=MESH)
        return carry

    for step in range(1, 8):
        pl.semaphore_signal(barrier, inc=1, device_id=(row, (col + step) % 8), device_id_type=MESH)
    lax.fori_loop(1, 16, greet, 0)

    pltpu.make_async_copy(lsep_h, lcol.at[z, y], s_own).start()
    pltpu.make_async_copy(usep_h, urow.at[k, x], s_own).start()
    pltpu.make_async_copy(rsep_h, rsep, s_own).start()

    def factors():
        pl.semaphore_wait(barrier, 22)
        for step in range(1, 8):
            pl.semaphore_signal(sem_a, inc=1, device_id=(row, (col + step) % 8), device_id_type=MESH)
        wait_kib(192, s_own)
        for step in (2, 1, 3):
            for cl in range(2):
                ref = lcol.at[z, y, pl.ds(64 * cl, 64)]
                remote(ref, ref, l_recv, along(cl, step)).start()
            remote(urow.at[k, x], urow.at[k, x], u_recv, along_x(step)).start()

    total = None
    before = None
    wait_bytes(sizes, s_sizes)
    for i in range(NT):
        span = pl.ds(0, TB * (i + 1))
        wait_kib(64 * (2 * i + 7), s_front.at[i % WINDOW])
        if i + WINDOW < NT:
            load_front(i + WINDOW)
        mask = keep(TB * i, TB, NR)
        rhs[rows_of(i), :] = jnp.where(mask, rhs[rows_of(i), :].astype(F32), 0.0).astype(BF)
        val = dot(linv[rows_of(i), span], rhs[span, :])
        val = jnp.where(mask, val, 0.0).astype(BF)
        mix[rows_of(i), pl.ds(KB * BLK, NR)] = val
        if before is not None:
            term = dot(loff[:, rows_of(i - 1)], before)
            total = term if total is None else total + term
        before = val
        if i == EARLY:
            factors()

    total = total + dot(loff[:, rows_of(NT - 1)], before)
    pltpu.make_async_copy(
        uoff_h.at[0], mix.at[:, pl.ds(0, KB * BLK)], s_back).start()
    for i in range(NT):
        span = pl.ds(TB * i, W - TB * i)
        pltpu.make_async_copy(
            uinv_h.at[0, rows_of(i), span], uinv.at[rows_of(i), span], s_back).start()

    for j in range(KB):
        upd[j] = total[BLK * j:BLK * (j + 1), :].reshape(8, 16, NR).astype(BF)
    upd[KB] = jnp.zeros((8, 16, NR), BF)
    wait_bytes(offs, s_offs)
    named = [offs[0, j] for j in range(KB)]

    def block(s):
        at = jnp.int32(KB)
        for j in range(KB):
            at = jnp.where(named[j] == s, j, at)
        return upd[at]

    swaps = []
    for j in range(4):
        c4 = (x + 2 + j) % 4
        for b in range(2):
            half[j, pl.ds(8 * b, 8)] = block(4 * c4 + 2 * other + b)
        swaps.append(remote(half.at[j], recv_half.at[j], swap_recv.at[j], partner))
        swaps[-1].start()
    pl.semaphore_wait(sem_a, 7)
    for j in range(4):
        c4 = (x + 2 + j) % 4
        swaps[j].wait_recv()
        for b in range(2):
            mine = block(4 * c4 + 2 * k + b).astype(F32)
            got = recv_half[j, pl.ds(8 * b, 8)].astype(F32)
            pieces[c4, pl.ds(8 * b, 8)] = (mine + got).astype(BF)

        def rs_body(i, carry, c4=c4):
            prow = ((z + i // 4 + 2) % 4) * 4 + (y + i + 2) % 4
            remote(pieces.at[c4, prow], rs_in.at[chip], rs_recv, (prow, c4 * 2 + k)).start()
            return carry

        if j == 2:
            lax.fori_loop(0, 10, rs_body, 0)
            lax.fori_loop(11, 16, rs_body, 0)
            rs_in[chip] = pieces[c4, row]
        else:
            lax.fori_loop(0, 16, rs_body, 0)

    def unit(cl, at, h):
        if cl == 0:
            return lcol.at[at, pl.ds(2 * h, 2), pl.ds(0, 64)]
        return lcol.at[pl.ds(2 * h, 2), at, pl.ds(64, 64)]

    def place(cl, step):
        return ((z if cl == 0 else y) + step) % 4

    wait_kib(192, l_recv)
    for d, h in ((0, 0), (1, 1), (0, 1), (1, 0)):
        for cl in range(2):
            ref = unit(cl, place(cl, 0), h)
            remote(ref, ref, near_recv if d == h else m_recv, along(1 - cl, 1 + 2 * d)).start()

    wait_kib(192, u_recv)
    remote(urow.at[k], urow.at[k], m_recv, partner).start()

    wait_kib(36 * 128 + 2048, s_back)
    for i in range(NT):
        val = mix[rows_of(i), pl.ds(0, KB * BLK)].astype(F32)
        mix[rows_of(i), pl.ds(0, KB * BLK)] = jnp.where(keep(TB * i, TB, KB * BLK), val, 0.0).astype(BF)

    def back(i):
        span = pl.ds(TB * i, W - TB * i)
        val = dot(uinv[rows_of(i), span], mix[span, pl.ds(0, KB * BLK)])
        gmat[rows_of(i), :] = jnp.where(keep(TB * i, TB, KB * BLK), val, 0.0).astype(BF)
        val = dot(uinv[rows_of(i), span], mix[span, pl.ds(KB * BLK, NR)])
        fsol[rows_of(i), :] = jnp.where(keep(TB * i, TB, NR), val, 0.0)

    back(0)
    back(1)
    wait_kib(256, near_recv)
    for d in range(2):
        for cl in range(2):
            ref = unit(cl, place(cl, 3 - 2 * d), d)
            remote(ref, ref, m_recv, along(1 - cl, 1 + 2 * d)).start()

    wait_bytes(rs_in.at[pl.ds(0, 63)], rs_recv)
    gathered = jnp.sum(rs_in[...].astype(F32), axis=0)
    xs[row] = (rsep[pl.ds(pl.multiple_of(row * 16, 16), 16), :].astype(F32) - gathered).astype(BF)

    for dz, dy in FAR_PLANE:
        remote(xs.at[row], xs.at[row], ag_recv, (((z + dz) % 4) * 4 + (y + dy) % 4, col)).start()
    for i in range(2, 5):
        back(i)

    wait_kib(768, m_recv)
    macc[...] = jnp.zeros_like(macc)

    def m_body(c, carry):
        macc[...] += dot(urow[c % 2, c // 2], lcol[c // 2, pl.ds(2 * (c % 2), 2)].reshape(TB, TB))
        return carry

    lax.fori_loop(jnp.maximum(col, row // 2), 8, m_body, 0)
    factor = macc[...].astype(BF)
    wait_bytes(xs.at[pl.ds(0, 15)], ag_recv)
    part[...] = dot(factor, xs[...].reshape(TB, NR)).reshape(8, 16, NR)

    for step in (4, 5, 3, 2, 6, 7, 1):
        to = (col + step) % 8
        remote(part.at[to], part_in.at[col], p_recv, (row, to)).start()
    part_in[col] = part[col]
    wait_bytes(part.at[pl.ds(0, 7)], p_recv)
    sol[k, row, x] = jnp.sum(part_in[...], axis=0).astype(BF)

    mine = sol.at[k, row, x]

    def sol_body(i, carry):
        pz, py, px = (z + i // 16 + 2) % 4, (y + i // 4 + 2) % 4, (x + i + 2) % 4
        remote(mine, mine, sol_recv.at[z], (pz * 4 + py, px * 2 + k)).start()
        return carry

    lax.fori_loop(0, 42, sol_body, 0)
    lax.fori_loop(43, 64, sol_body, 0)
    for i in range(5, NT):
        back(i)
    for step in (0, 1, 3, 2):
        pz = (z + step) % 4
        wait_bytes(rs_in.at[pl.ds(0, 16 if step else 15)], sol_recv.at[pz])
        ref = sol.at[k, pl.ds(4 * pz, 4)]
        remote(ref, ref, last_recv, partner).start()
    wait_kib(256, last_recv)

    for j in range(KB):
        for h in range(2):
            got = sol[h, named[j]]
            for q in range(4):
                coupled[pl.ds(BLK * j + 32 * q + 16 * h, 16), :] = got[q]
    for h in range(2):
        got = sol[h, row]
        for q in range(4):
            osep[pl.ds(32 * q + 16 * h, 16), :] = got[q]

    wait_kib(2496, s_send)
    wait_bytes(fsol.at[pl.ds(0, 88)], s_send)


def finish(gmat, fsol, coupled, sep, leaf_out, sep_out, leaf, sems):
    copies = [pltpu.make_async_copy(sep, sep_out, sems.at[0])]
    copies[0].start()
    for i in range(0, NT, 2):
        rows = pl.ds(TB * i, 2 * TB)
        leaf[rows, :] = (fsol[rows, :] - dot(gmat[rows, :], coupled[...])).astype(BF)
        copies.append(pltpu.make_async_copy(leaf.at[rows], leaf_out.at[0, rows], sems.at[1 + i // 2]))
        copies[-1].start()
    for copy in copies:
        copy.wait()


def shards(
    rhs_leaf, rhs_sep, leaf_sizes, off_blocks, linv_leaf, uinv_leaf, l_off, u_off, linv_sep, uinv_sep,
):
    any_spec = pl.BlockSpec(memory_space=pl.ANY)
    dma = pltpu.SemaphoreType.DMA
    vm = pltpu.VMEM
    solved = pl.pallas_call(
        kernel,
        out_shape=(vm((W, KB * BLK), BF), vm((W, NR), F32), vm((KB * BLK, NR), BF), vm((BLK, NR), BF)),
        in_specs=[any_spec] * 10,
        out_specs=(pl.BlockSpec(memory_space=vm),) * 4,
        scratch_shapes=[
            vm((W, W), BF), vm((W, W), BF), vm((KB * BLK, W), BF), vm((W, NR), BF),
            vm((W, KB * BLK + NR), BF),
            vm((KB + 1, 8, 16, NR), BF), vm((TB, NR), BF),
            vm((4, 4, BLK, TB), BF), vm((2, 4, BLK, TB), BF), vm((BLK, TB), F32),
            vm((4, 16, 16, NR), BF), vm((4, 16, 16, NR), BF), vm((4, 16, 16, NR), BF),
            vm((64, 16, NR), BF), vm((16, 16, NR), BF),
            vm((8, 16, NR), F32), vm((8, 16, NR), F32), vm((2, 16, 4, 16, NR), BF),
            dma((WINDOW,)), dma, dma, dma, dma, dma, dma, dma, dma,
            dma((4,)), dma, dma, dma, dma((4,)),
            pltpu.SemaphoreType.REGULAR, pltpu.SMEM((1,), jnp.int32), pltpu.SMEM((1, KB), jnp.int32), dma, dma,
        ],
        compiler_params=pltpu.CompilerParams(
            collective_id=0, has_side_effects=True, vmem_limit_bytes=56 * 1024 * 1024),
        name="supernodal_solve",
    )(leaf_sizes, off_blocks, rhs_leaf, rhs_sep, linv_leaf, uinv_leaf, l_off, u_off, linv_sep, uinv_sep)
    return pl.pallas_call(
        finish,
        out_shape=(jax.ShapeDtypeStruct((1, W, NR), BF), jax.ShapeDtypeStruct((BLK, NR), BF)),
        in_specs=[pl.BlockSpec(memory_space=vm)] * 4,
        out_specs=(any_spec, any_spec),
        scratch_shapes=[vm((W, NR), BF), dma((1 + NT // 2,))],
        compiler_params=pltpu.CompilerParams(vmem_limit_bytes=8 * 1024 * 1024),
        name="leaf_finish",
    )(*solved)


def solution(mesh):
    placed = (
        P(("row", "col"), None, None),
        P("col", None),
        P(("row", "col")),
        P(("row", "col"), None),
        P(("row", "col"), None, None),
        P(("row", "col"), None, None),
        P(("row", "col"), None, None),
        P(("row", "col"), None, None),
        P("row", "col"),
        P("row", "col"),
    )
    return jax.shard_map(
        shards,
        mesh=mesh,
        in_specs=placed,
        out_specs=(P(("row", "col"), None, None), P("row", None)),
        check_vma=False,
    )
```

```python
import jax
import jax.numpy as jnp
from jax import lax
from jax.experimental import pallas as pl
from jax.experimental.pallas import tpu as pltpu
from jax.sharding import PartitionSpec as P

MESH = pl.DeviceIdType.MESH
W = 2048
NR = 128
BLK = 128
KB = 4
TB = 256
NT = W // TB
WINDOW = 4
EARLY = 4
FAR_PLANE = sorted(
    [(i // 4, i % 4) for i in range(1, 16)],
    key=lambda d: -(min(d[0], 4 - d[0]) + min(d[1], 4 - d[1])))
BF = jnp.bfloat16
F32 = jnp.float32


def dot(a, b):
    return jnp.dot(a, b, preferred_element_type=F32)


def kernel(
    sizes_h, offs_h, rhs_h, rsep_h, linv_h, uinv_h, loff_h, uoff_h, lsep_h, usep_h,
    gmat, fsol, coupled, osep,
    linv, uinv, loff, rhs, mix, upd, rsep,
    lcol, urow, macc,
    half, recv_half, pieces, rs_in, xs, part, part_in, sol,
    s_front, s_back, s_own, s_send, l_recv, u_recv, near_recv, m_recv, p_recv,
    swap_recv, last_recv, rs_recv, ag_recv, sol_recv,
    sem_a, sizes, offs, s_sizes, s_offs,
):
    row, col = lax.axis_index("row"), lax.axis_index("col")
    z, y = row // 4, row % 4
    x, k = col // 2, col % 2
    other = 1 - k
    chip = z * 16 + y * 4 + x
    partner = (row, x * 2 + other)

    def along_x(step):
        return (row, ((x + step) % 4) * 2 + k)

    def along(cl, step):
        if cl == 0:
            return (z * 4 + (y + step) % 4, col)
        return (((z + step) % 4) * 4 + y, col)

    def wait_bytes(ref, sem):
        pltpu.make_async_copy(ref, ref, sem).wait()

    def wait_kib(count, sem):
        wait_bytes(linv.at[pl.ds(0, count // 4)], sem)

    def remote(src, dst, recv, device):
        return pltpu.make_async_remote_copy(
            src_ref=src, dst_ref=dst, send_sem=s_send, recv_sem=recv,
            device_id=device, device_id_type=MESH)

    def keep(start, rows, cols):
        return lax.broadcasted_iota(jnp.int32, (rows, cols), 0) + start < sizes[0]

    def rows_of(i):
        return pl.ds(TB * i, TB)

    def load_front(i):
        pltpu.make_async_copy(rhs_h.at[0, rows_of(i)], rhs.at[rows_of(i)], s_front.at[i % WINDOW]).start()
        span = pl.ds(0, TB * (i + 1))
        pltpu.make_async_copy(
            linv_h.at[0, rows_of(i), span], linv.at[rows_of(i), span], s_front.at[i % WINDOW]).start()
        pltpu.make_async_copy(
            loff_h.at[0, :, rows_of(i)], loff.at[:, rows_of(i)], s_front.at[i % WINDOW]).start()

    pltpu.make_async_copy(sizes_h, sizes, s_sizes).start()
    for i in range(WINDOW):
        load_front(i)
    pltpu.make_async_copy(offs_h, offs, s_offs).start()

    barrier = pltpu.get_barrier_semaphore()

    def greet(i, carry):
        pl.semaphore_signal(barrier, inc=1, device_id=((row + i) % 16, col), device_id_type=MESH)
        return carry

    for step in range(1, 8):
        pl.semaphore_signal(barrier, inc=1, device_id=(row, (col + step) % 8), device_id_type=MESH)
    lax.fori_loop(1, 16, greet, 0)

    pltpu.make_async_copy(lsep_h, lcol.at[z, y], s_own).start()
    pltpu.make_async_copy(usep_h, urow.at[k, x], s_own).start()
    pltpu.make_async_copy(rsep_h, rsep, s_own).start()

    def factors():
        pl.semaphore_wait(barrier, 22)
        for step in range(1, 8):
            pl.semaphore_signal(sem_a, inc=1, device_id=(row, (col + step) % 8), device_id_type=MESH)
        wait_kib(192, s_own)
        for step in (2, 1, 3):
            for cl in range(2):
                ref = lcol.at[z, y, pl.ds(64 * cl, 64)]
                remote(ref, ref, l_recv, along(cl, step)).start()
            remote(urow.at[k, x], urow.at[k, x], u_recv, along_x(step)).start()

    total = None
    before = None
    wait_bytes(sizes, s_sizes)
    for i in range(NT):
        span = pl.ds(0, TB * (i + 1))
        wait_kib(64 * (2 * i + 7), s_front.at[i % WINDOW])
        if i + WINDOW < NT:
            load_front(i + WINDOW)
        mask = keep(TB * i, TB, NR)
        rhs[rows_of(i), :] = jnp.where(mask, rhs[rows_of(i), :].astype(F32), 0.0).astype(BF)
        val = dot(linv[rows_of(i), span], rhs[span, :])
        val = jnp.where(mask, val, 0.0).astype(BF)
        mix[rows_of(i), pl.ds(KB * BLK, NR)] = val
        if before is not None:
            term = dot(loff[:, rows_of(i - 1)], before)
            total = term if total is None else total + term
        before = val
        if i == EARLY:
            factors()

    total = total + dot(loff[:, rows_of(NT - 1)], before)
    pltpu.make_async_copy(
        uoff_h.at[0], mix.at[:, pl.ds(0, KB * BLK)], s_back).start()
    for i in range(NT):
        span = pl.ds(TB * i, W - TB * i)
        pltpu.make_async_copy(
            uinv_h.at[0, rows_of(i), span], uinv.at[rows_of(i), span], s_back).start()

    for j in range(KB):
        upd[j] = total[BLK * j:BLK * (j + 1), :].reshape(8, 16, NR).astype(BF)
    upd[KB] = jnp.zeros((8, 16, NR), BF)
    wait_bytes(offs, s_offs)
    named = [offs[0, j] for j in range(KB)]

    def block(s):
        at = jnp.int32(KB)
        for j in range(KB):
            at = jnp.where(named[j] == s, j, at)
        return upd[at]

    swaps = []
    for j in range(4):
        c4 = (x + 2 + j) % 4
        for b in range(2):
            half[j, pl.ds(8 * b, 8)] = block(4 * c4 + 2 * other + b)
        swaps.append(remote(half.at[j], recv_half.at[j], swap_recv.at[j], partner))
        swaps[-1].start()
    pl.semaphore_wait(sem_a, 7)
    for j in range(4):
        c4 = (x + 2 + j) % 4
        swaps[j].wait_recv()
        for b in range(2):
            mine = block(4 * c4 + 2 * k + b).astype(F32)
            got = recv_half[j, pl.ds(8 * b, 8)].astype(F32)
            pieces[c4, pl.ds(8 * b, 8)] = (mine + got).astype(BF)

        def rs_body(i, carry, c4=c4):
            prow = ((z + i // 4 + 2) % 4) * 4 + (y + i + 2) % 4
            remote(pieces.at[c4, prow], rs_in.at[chip], rs_recv, (prow, c4 * 2 + k)).start()
            return carry

        if j == 2:
            lax.fori_loop(0, 10, rs_body, 0)
            lax.fori_loop(11, 16, rs_body, 0)
            rs_in[chip] = pieces[c4, row]
        else:
            lax.fori_loop(0, 16, rs_body, 0)

    def unit(cl, at, h):
        if cl == 0:
            return lcol.at[at, pl.ds(2 * h, 2), pl.ds(0, 64)]
        return lcol.at[pl.ds(2 * h, 2), at, pl.ds(64, 64)]

    def place(cl, step):
        return ((z if cl == 0 else y) + step) % 4

    wait_kib(192, l_recv)
    for d, h in ((0, 0), (1, 1), (0, 1), (1, 0)):
        for cl in range(2):
            ref = unit(cl, place(cl, 0), h)
            remote(ref, ref, near_recv if d == h else m_recv, along(1 - cl, 1 + 2 * d)).start()

    wait_kib(192, u_recv)
    remote(urow.at[k], urow.at[k], m_recv, partner).start()

    wait_kib(36 * 128 + 2048, s_back)
    for i in range(NT):
        val = mix[rows_of(i), pl.ds(0, KB * BLK)].astype(F32)
        mix[rows_of(i), pl.ds(0, KB * BLK)] = jnp.where(keep(TB * i, TB, KB * BLK), val, 0.0).astype(BF)

    def back(i):
        span = pl.ds(TB * i, W - TB * i)
        val = dot(uinv[rows_of(i), span], mix[span, pl.ds(0, KB * BLK)])
        gmat[rows_of(i), :] = jnp.where(keep(TB * i, TB, KB * BLK), val, 0.0).astype(BF)
        val = dot(uinv[rows_of(i), span], mix[span, pl.ds(KB * BLK, NR)])
        fsol[rows_of(i), :] = jnp.where(keep(TB * i, TB, NR), val, 0.0)

    back(0)
    back(1)
    wait_bytes(rs_in.at[pl.ds(0, 63)], rs_recv)
    gathered = jnp.sum(rs_in[...].astype(F32), axis=0)
    xs[row] = (rsep[pl.ds(pl.multiple_of(row * 16, 16), 16), :].astype(F32) - gathered).astype(BF)

    for dz, dy in FAR_PLANE:
        remote(xs.at[row], xs.at[row], ag_recv, (((z + dz) % 4) * 4 + (y + dy) % 4, col)).start()
    wait_kib(256, near_recv)
    for d in range(2):
        for cl in range(2):
            ref = unit(cl, place(cl, 3 - 2 * d), d)
            remote(ref, ref, m_recv, along(1 - cl, 1 + 2 * d)).start()
    for i in range(2, 5):
        back(i)

    wait_kib(768, m_recv)
    macc[...] = jnp.zeros_like(macc)

    def m_body(c, carry):
        macc[...] += dot(urow[c % 2, c // 2], lcol[c // 2, pl.ds(2 * (c % 2), 2)].reshape(TB, TB))
        return carry

    lax.fori_loop(jnp.maximum(col, row // 2), 8, m_body, 0)
    factor = macc[...].astype(BF)
    wait_bytes(xs.at[pl.ds(0, 15)], ag_recv)
    part[...] = dot(factor, xs[...].reshape(TB, NR)).reshape(8, 16, NR)

    for step in (4, 5, 3, 2, 6, 7, 1):
        to = (col + step) % 8
        remote(part.at[to], part_in.at[col], p_recv, (row, to)).start()
    part_in[col] = part[col]
    wait_bytes(part.at[pl.ds(0, 7)], p_recv)
    sol[k, row, x] = jnp.sum(part_in[...], axis=0).astype(BF)

    mine = sol.at[k, row, x]

    def sol_body(i, carry):
        pz, py, px = (z + i // 16 + 2) % 4, (y + i // 4 + 2) % 4, (x + i + 2) % 4
        remote(mine, mine, sol_recv.at[z], (pz * 4 + py, px * 2 + k)).start()
        return carry

    lax.fori_loop(0, 42, sol_body, 0)
    lax.fori_loop(43, 64, sol_body, 0)
    for i in range(5, NT):
        back(i)
    for step in (0, 1, 3, 2):
        pz = (z + step) % 4
        wait_bytes(rs_in.at[pl.ds(0, 16 if step else 15)], sol_recv.at[pz])
        ref = sol.at[k, pl.ds(4 * pz, 4)]
        remote(ref, ref, last_recv, partner).start()
    wait_kib(256, last_recv)

    for j in range(KB):
        for h in range(2):
            got = sol[h, named[j]]
            for q in range(4):
                coupled[pl.ds(BLK * j + 32 * q + 16 * h, 16), :] = got[q]
    for h in range(2):
        got = sol[h, row]
        for q in range(4):
            osep[pl.ds(32 * q + 16 * h, 16), :] = got[q]

    wait_kib(2496, s_send)
    wait_bytes(fsol.at[pl.ds(0, 88)], s_send)


def finish(gmat, fsol, coupled, sep, leaf_out, sep_out, leaf, sems):
    copies = [pltpu.make_async_copy(sep, sep_out, sems.at[0])]
    copies[0].start()
    for i in range(0, NT, 2):
        rows = pl.ds(TB * i, 2 * TB)
        leaf[rows, :] = (fsol[rows, :] - dot(gmat[rows, :], coupled[...])).astype(BF)
        copies.append(pltpu.make_async_copy(leaf.at[rows], leaf_out.at[0, rows], sems.at[1 + i // 2]))
        copies[-1].start()
    for copy in copies:
        copy.wait()


def shards(
    rhs_leaf, rhs_sep, leaf_sizes, off_blocks, linv_leaf, uinv_leaf, l_off, u_off, linv_sep, uinv_sep,
):
    any_spec = pl.BlockSpec(memory_space=pl.ANY)
    dma = pltpu.SemaphoreType.DMA
    vm = pltpu.VMEM
    solved = pl.pallas_call(
        kernel,
        out_shape=(vm((W, KB * BLK), BF), vm((W, NR), F32), vm((KB * BLK, NR), BF), vm((BLK, NR), BF)),
        in_specs=[any_spec] * 10,
        out_specs=(pl.BlockSpec(memory_space=vm),) * 4,
        scratch_shapes=[
            vm((W, W), BF), vm((W, W), BF), vm((KB * BLK, W), BF), vm((W, NR), BF),
            vm((W, KB * BLK + NR), BF),
            vm((KB + 1, 8, 16, NR), BF), vm((TB, NR), BF),
            vm((4, 4, BLK, TB), BF), vm((2, 4, BLK, TB), BF), vm((BLK, TB), F32),
            vm((4, 16, 16, NR), BF), vm((4, 16, 16, NR), BF), vm((4, 16, 16, NR), BF),
            vm((64, 16, NR), BF), vm((16, 16, NR), BF),
            vm((8, 16, NR), F32), vm((8, 16, NR), F32), vm((2, 16, 4, 16, NR), BF),
            dma((WINDOW,)), dma, dma, dma, dma, dma, dma, dma, dma,
            dma((4,)), dma, dma, dma, dma((4,)),
            pltpu.SemaphoreType.REGULAR, pltpu.SMEM((1,), jnp.int32), pltpu.SMEM((1, KB), jnp.int32), dma, dma,
        ],
        compiler_params=pltpu.CompilerParams(
            collective_id=0, has_side_effects=True, vmem_limit_bytes=56 * 1024 * 1024),
        name="supernodal_solve",
    )(leaf_sizes, off_blocks, rhs_leaf, rhs_sep, linv_leaf, uinv_leaf, l_off, u_off, linv_sep, uinv_sep)
    return pl.pallas_call(
        finish,
        out_shape=(jax.ShapeDtypeStruct((1, W, NR), BF), jax.ShapeDtypeStruct((BLK, NR), BF)),
        in_specs=[pl.BlockSpec(memory_space=vm)] * 4,
        out_specs=(any_spec, any_spec),
        scratch_shapes=[vm((W, NR), BF), dma((1 + NT // 2,))],
        compiler_params=pltpu.CompilerParams(vmem_limit_bytes=8 * 1024 * 1024),
        name="leaf_finish",
    )(*solved)


def solution(mesh):
    placed = (
        P(("row", "col"), None, None),
        P("col", None),
        P(("row", "col")),
        P(("row", "col"), None),
        P(("row", "col"), None, None),
        P(("row", "col"), None, None),
        P(("row", "col"), None, None),
        P(("row", "col"), None, None),
        P("row", "col"),
        P("row", "col"),
    )
    return jax.shard_map(
        shards,
        mesh=mesh,
        in_specs=placed,
        out_specs=(P(("row", "col"), None, None), P("row", None)),
        check_vma=False,
    )
```

```python
import jax
import jax.numpy as jnp
from jax import lax
from jax.experimental import pallas as pl
from jax.experimental.pallas import tpu as pltpu
from jax.sharding import PartitionSpec as P

MESH = pl.DeviceIdType.MESH
W = 2048
NR = 128
BLK = 128
KB = 4
TB = 256
NT = W // TB
WINDOW = 4
EARLY = 3
FAR_PLANE = sorted(
    [(i // 4, i % 4) for i in range(1, 16)],
    key=lambda d: -(min(d[0], 4 - d[0]) + min(d[1], 4 - d[1])))
BF = jnp.bfloat16
F32 = jnp.float32


def dot(a, b):
    return jnp.dot(a, b, preferred_element_type=F32)


def kernel(
    sizes_h, offs_h, rhs_h, rsep_h, linv_h, uinv_h, loff_h, uoff_h, lsep_h, usep_h,
    gmat, fsol, coupled, osep,
    linv, uinv, loff, rhs, mix, upd, rsep,
    lcol, urow, macc,
    half, recv_half, pieces, rs_in, xs, part, part_in, sol,
    s_front, s_back, s_own, s_send, l_recv, u_recv, near_recv, m_recv, p_recv,
    swap_recv, last_recv, rs_recv, ag_recv, sol_recv,
    sem_a, sizes, offs, s_sizes, s_offs,
):
    row, col = lax.axis_index("row"), lax.axis_index("col")
    z, y = row // 4, row % 4
    x, k = col // 2, col % 2
    other = 1 - k
    chip = z * 16 + y * 4 + x
    partner = (row, x * 2 + other)

    def along_x(step):
        return (row, ((x + step) % 4) * 2 + k)

    def along(cl, step):
        if cl == 0:
            return (z * 4 + (y + step) % 4, col)
        return (((z + step) % 4) * 4 + y, col)

    def wait_bytes(ref, sem):
        pltpu.make_async_copy(ref, ref, sem).wait()

    def wait_kib(count, sem):
        wait_bytes(linv.at[pl.ds(0, count // 4)], sem)

    def remote(src, dst, recv, device):
        return pltpu.make_async_remote_copy(
            src_ref=src, dst_ref=dst, send_sem=s_send, recv_sem=recv,
            device_id=device, device_id_type=MESH)

    def keep(start, rows, cols):
        return lax.broadcasted_iota(jnp.int32, (rows, cols), 0) + start < sizes[0]

    def rows_of(i):
        return pl.ds(TB * i, TB)

    def load_front(i):
        pltpu.make_async_copy(rhs_h.at[0, rows_of(i)], rhs.at[rows_of(i)], s_front.at[i % WINDOW]).start()
        span = pl.ds(0, TB * (i + 1))
        pltpu.make_async_copy(
            linv_h.at[0, rows_of(i), span], linv.at[rows_of(i), span], s_front.at[i % WINDOW]).start()
        pltpu.make_async_copy(
            loff_h.at[0, :, rows_of(i)], loff.at[:, rows_of(i)], s_front.at[i % WINDOW]).start()

    pltpu.make_async_copy(sizes_h, sizes, s_sizes).start()
    for i in range(WINDOW):
        load_front(i)
    pltpu.make_async_copy(offs_h, offs, s_offs).start()

    barrier = pltpu.get_barrier_semaphore()

    def greet(i, carry):
        pl.semaphore_signal(barrier, inc=1, device_id=((row + i) % 16, col), device_id_type=MESH)
        return carry

    for step in range(1, 8):
        pl.semaphore_signal(barrier, inc=1, device_id=(row, (col + step) % 8), device_id_type=MESH)
    lax.fori_loop(1, 16, greet, 0)

    pltpu.make_async_copy(lsep_h, lcol.at[z, y], s_own).start()
    pltpu.make_async_copy(usep_h, urow.at[k, x], s_own).start()
    pltpu.make_async_copy(rsep_h, rsep, s_own).start()

    def factors():
        pl.semaphore_wait(barrier, 22)
        for step in range(1, 8):
            pl.semaphore_signal(sem_a, inc=1, device_id=(row, (col + step) % 8), device_id_type=MESH)
        wait_kib(192, s_own)
        for step in (2, 1, 3):
            for cl in range(2):
                ref = lcol.at[z, y, pl.ds(64 * cl, 64)]
                remote(ref, ref, l_recv, along(cl, step)).start()
            remote(urow.at[k, x], urow.at[k, x], u_recv, along_x(step)).start()

    total = None
    before = None
    wait_bytes(sizes, s_sizes)
    for i in range(NT):
        span = pl.ds(0, TB * (i + 1))
        wait_kib(64 * (2 * i + 7), s_front.at[i % WINDOW])
        if i + WINDOW < NT:
            load_front(i + WINDOW)
        mask = keep(TB * i, TB, NR)
        rhs[rows_of(i), :] = jnp.where(mask, rhs[rows_of(i), :].astype(F32), 0.0).astype(BF)
        val = dot(linv[rows_of(i), span], rhs[span, :])
        val = jnp.where(mask, val, 0.0).astype(BF)
        mix[rows_of(i), pl.ds(KB * BLK, NR)] = val
        if before is not None:
            term = dot(loff[:, rows_of(i - 1)], before)
            total = term if total is None else total + term
        before = val
        if i == EARLY:
            factors()

    total = total + dot(loff[:, rows_of(NT - 1)], before)
    pltpu.make_async_copy(
        uoff_h.at[0], mix.at[:, pl.ds(0, KB * BLK)], s_back).start()
    for i in range(NT):
        span = pl.ds(TB * i, W - TB * i)
        pltpu.make_async_copy(
            uinv_h.at[0, rows_of(i), span], uinv.at[rows_of(i), span], s_back).start()

    for j in range(KB):
        upd[j] = total[BLK * j:BLK * (j + 1), :].reshape(8, 16, NR).astype(BF)
    upd[KB] = jnp.zeros((8, 16, NR), BF)
    wait_bytes(offs, s_offs)
    named = [offs[0, j] for j in range(KB)]

    def block(s):
        at = jnp.int32(KB)
        for j in range(KB):
            at = jnp.where(named[j] == s, j, at)
        return upd[at]

    swaps = []
    for j in range(4):
        c4 = (x + 2 + j) % 4
        for b in range(2):
            half[j, pl.ds(8 * b, 8)] = block(4 * c4 + 2 * other + b)
        swaps.append(remote(half.at[j], recv_half.at[j], swap_recv.at[j], partner))
        swaps[-1].start()
    pl.semaphore_wait(sem_a, 7)
    for j in range(4):
        c4 = (x + 2 + j) % 4
        swaps[j].wait_recv()
        for b in range(2):
            mine = block(4 * c4 + 2 * k + b).astype(F32)
            got = recv_half[j, pl.ds(8 * b, 8)].astype(F32)
            pieces[c4, pl.ds(8 * b, 8)] = (mine + got).astype(BF)

        def rs_body(i, carry, c4=c4):
            prow = ((z + i // 4 + 2) % 4) * 4 + (y + i + 2) % 4
            remote(pieces.at[c4, prow], rs_in.at[chip], rs_recv, (prow, c4 * 2 + k)).start()
            return carry

        if j == 2:
            lax.fori_loop(0, 10, rs_body, 0)
            lax.fori_loop(11, 16, rs_body, 0)
            rs_in[chip] = pieces[c4, row]
        else:
            lax.fori_loop(0, 16, rs_body, 0)

    def unit(cl, at, h):
        if cl == 0:
            return lcol.at[at, pl.ds(2 * h, 2), pl.ds(0, 64)]
        return lcol.at[pl.ds(2 * h, 2), at, pl.ds(64, 64)]

    def place(cl, step):
        return ((z if cl == 0 else y) + step) % 4

    wait_kib(192, l_recv)
    for d, h in ((0, 0), (1, 1), (0, 1), (1, 0)):
        for cl in range(2):
            ref = unit(cl, place(cl, 0), h)
            remote(ref, ref, near_recv if d == h else m_recv, along(1 - cl, 1 + 2 * d)).start()

    wait_kib(192, u_recv)
    remote(urow.at[k], urow.at[k], m_recv, partner).start()

    wait_kib(36 * 128 + 2048, s_back)
    for i in range(NT):
        val = mix[rows_of(i), pl.ds(0, KB * BLK)].astype(F32)
        mix[rows_of(i), pl.ds(0, KB * BLK)] = jnp.where(keep(TB * i, TB, KB * BLK), val, 0.0).astype(BF)

    def back(i):
        span = pl.ds(TB * i, W - TB * i)
        val = dot(uinv[rows_of(i), span], mix[span, pl.ds(0, KB * BLK)])
        gmat[rows_of(i), :] = jnp.where(keep(TB * i, TB, KB * BLK), val, 0.0).astype(BF)
        val = dot(uinv[rows_of(i), span], mix[span, pl.ds(KB * BLK, NR)])
        fsol[rows_of(i), :] = jnp.where(keep(TB * i, TB, NR), val, 0.0)

    back(0)
    back(1)
    wait_bytes(rs_in.at[pl.ds(0, 63)], rs_recv)
    gathered = jnp.sum(rs_in[...].astype(F32), axis=0)
    xs[row] = (rsep[pl.ds(pl.multiple_of(row * 16, 16), 16), :].astype(F32) - gathered).astype(BF)

    for dz, dy in FAR_PLANE:
        remote(xs.at[row], xs.at[row], ag_recv, (((z + dz) % 4) * 4 + (y + dy) % 4, col)).start()
    wait_kib(256, near_recv)
    for d in range(2):
        for cl in range(2):
            ref = unit(cl, place(cl, 3 - 2 * d), d)
            remote(ref, ref, m_recv, along(1 - cl, 1 + 2 * d)).start()
    for i in range(2, 5):
        back(i)

    wait_kib(768, m_recv)
    macc[...] = jnp.zeros_like(macc)

    def m_body(c, carry):
        macc[...] += dot(urow[c % 2, c // 2], lcol[c // 2, pl.ds(2 * (c % 2), 2)].reshape(TB, TB))
        return carry

    lax.fori_loop(jnp.maximum(col, row // 2), 8, m_body, 0)
    factor = macc[...].astype(BF)
    wait_bytes(xs.at[pl.ds(0, 15)], ag_recv)
    part[...] = dot(factor, xs[...].reshape(TB, NR)).reshape(8, 16, NR)

    for step in (4, 5, 3, 2, 6, 7, 1):
        to = (col + step) % 8
        remote(part.at[to], part_in.at[col], p_recv, (row, to)).start()
    part_in[col] = part[col]
    wait_bytes(part.at[pl.ds(0, 7)], p_recv)
    sol[k, row, x] = jnp.sum(part_in[...], axis=0).astype(BF)

    mine = sol.at[k, row, x]

    def sol_body(i, carry):
        pz, py, px = (z + i // 16 + 2) % 4, (y + i // 4 + 2) % 4, (x + i + 2) % 4
        remote(mine, mine, sol_recv.at[z], (pz * 4 + py, px * 2 + k)).start()
        return carry

    lax.fori_loop(0, 42, sol_body, 0)
    lax.fori_loop(43, 64, sol_body, 0)
    for i in range(5, NT):
        back(i)
    for step in (0, 1, 3, 2):
        pz = (z + step) % 4
        wait_bytes(rs_in.at[pl.ds(0, 16 if step else 15)], sol_recv.at[pz])
        ref = sol.at[k, pl.ds(4 * pz, 4)]
        remote(ref, ref, last_recv, partner).start()
    wait_kib(256, last_recv)

    for j in range(KB):
        for h in range(2):
            got = sol[h, named[j]]
            for q in range(4):
                coupled[pl.ds(BLK * j + 32 * q + 16 * h, 16), :] = got[q]
    for h in range(2):
        got = sol[h, row]
        for q in range(4):
            osep[pl.ds(32 * q + 16 * h, 16), :] = got[q]

    wait_kib(2496, s_send)
    wait_bytes(fsol.at[pl.ds(0, 88)], s_send)


def finish(gmat, fsol, coupled, sep, leaf_out, sep_out, leaf, sems):
    copies = [pltpu.make_async_copy(sep, sep_out, sems.at[0])]
    copies[0].start()
    for i in range(0, NT, 2):
        rows = pl.ds(TB * i, 2 * TB)
        leaf[rows, :] = (fsol[rows, :] - dot(gmat[rows, :], coupled[...])).astype(BF)
        copies.append(pltpu.make_async_copy(leaf.at[rows], leaf_out.at[0, rows], sems.at[1 + i // 2]))
        copies[-1].start()
    for copy in copies:
        copy.wait()


def shards(
    rhs_leaf, rhs_sep, leaf_sizes, off_blocks, linv_leaf, uinv_leaf, l_off, u_off, linv_sep, uinv_sep,
):
    any_spec = pl.BlockSpec(memory_space=pl.ANY)
    dma = pltpu.SemaphoreType.DMA
    vm = pltpu.VMEM
    solved = pl.pallas_call(
        kernel,
        out_shape=(vm((W, KB * BLK), BF), vm((W, NR), F32), vm((KB * BLK, NR), BF), vm((BLK, NR), BF)),
        in_specs=[any_spec] * 10,
        out_specs=(pl.BlockSpec(memory_space=vm),) * 4,
        scratch_shapes=[
            vm((W, W), BF), vm((W, W), BF), vm((KB * BLK, W), BF), vm((W, NR), BF),
            vm((W, KB * BLK + NR), BF),
            vm((KB + 1, 8, 16, NR), BF), vm((TB, NR), BF),
            vm((4, 4, BLK, TB), BF), vm((2, 4, BLK, TB), BF), vm((BLK, TB), F32),
            vm((4, 16, 16, NR), BF), vm((4, 16, 16, NR), BF), vm((4, 16, 16, NR), BF),
            vm((64, 16, NR), BF), vm((16, 16, NR), BF),
            vm((8, 16, NR), F32), vm((8, 16, NR), F32), vm((2, 16, 4, 16, NR), BF),
            dma((WINDOW,)), dma, dma, dma, dma, dma, dma, dma, dma,
            dma((4,)), dma, dma, dma, dma((4,)),
            pltpu.SemaphoreType.REGULAR, pltpu.SMEM((1,), jnp.int32), pltpu.SMEM((1, KB), jnp.int32), dma, dma,
        ],
        compiler_params=pltpu.CompilerParams(
            collective_id=0, has_side_effects=True, vmem_limit_bytes=56 * 1024 * 1024),
        name="supernodal_solve",
    )(leaf_sizes, off_blocks, rhs_leaf, rhs_sep, linv_leaf, uinv_leaf, l_off, u_off, linv_sep, uinv_sep)
    return pl.pallas_call(
        finish,
        out_shape=(jax.ShapeDtypeStruct((1, W, NR), BF), jax.ShapeDtypeStruct((BLK, NR), BF)),
        in_specs=[pl.BlockSpec(memory_space=vm)] * 4,
        out_specs=(any_spec, any_spec),
        scratch_shapes=[vm((W, NR), BF), dma((1 + NT // 2,))],
        compiler_params=pltpu.CompilerParams(vmem_limit_bytes=8 * 1024 * 1024),
        name="leaf_finish",
    )(*solved)


def solution(mesh):
    placed = (
        P(("row", "col"), None, None),
        P("col", None),
        P(("row", "col")),
        P(("row", "col"), None),
        P(("row", "col"), None, None),
        P(("row", "col"), None, None),
        P(("row", "col"), None, None),
        P(("row", "col"), None, None),
        P("row", "col"),
        P("row", "col"),
    )
    return jax.shard_map(
        shards,
        mesh=mesh,
        in_specs=placed,
        out_specs=(P(("row", "col"), None, None), P("row", None)),
        check_vma=False,
    )
```
